512 devices in a mesh: row: 16 (over y, x_hi), col: 32 (over x_lo, z, core).
Axes of the slice: x: 4 (x_hi: 2, x_lo: 2; x = x_hi * 2 + x_lo), y: 8, z: 8, core: 2. Of those that a mesh axis runs over, the one named last changes fastest.
Arguments:
- height: float32 [2048, 4096], P('row', 'col'), may hold values from -6 to 6
- density: float32 [2048, 4096], P('row', 'col'), may hold values from 0.2 to 1
- target: float32 [2048, 4096], P('row', 'col'), may hold values from -6 to 6
- region_of_block: int32 [16, 32], P('row', 'col'), may hold values from 0 to 127
- class_of_block: int32 [16, 32], P('row', 'col'), may hold values from 0 to 7
- fill_level: float32 [128], replicated, may hold values from 0 to 0.5
- rates: float32 [8], replicated, may hold values from 0.1 to 0.6
- col_taps: float32 [8, 33], replicated, may hold values from -1 to 1
- row_taps: float32 [8, 33], replicated, may hold values from -1 to 1
- gains: float32 [8], replicated, may hold values from 0.2 to 0.6
Outputs:
- new_height: float32 [2048, 4096], P('row', 'col')
- gain_grad: float32 [8], replicated
- fill_grad: float32 [128], replicated
The draws below stay inside these ranges and needn't reach their ends.
All inputs are finite; a program needn't handle non-finite values.
Results may differ from the reference program's by a relative error of at most 0.00035.
The reference program's roundings to bfloat16 on the way (of `source`, `col_kernel`, `row_kernel`, `smoothed`, `pressure_adjoint` and `weighted`) count: a program that leaves them out, or rounds other values in their place, can miss the bound.
Values may be sent and summed in bfloat16 or wider, within the bound.
No kernel may reach another device: no remote copies, remote signals or barrier semaphores. Data moves between devices by JAX's collectives and lax.ppermute only.
A program may use at most 128 MiB of HBM per device.

```python
import math
import jax
import jax.numpy as jnp
import numpy as np
from jax import lax

CHANNELS = 8
TAPS = 33
BLOCK = 128
NCLASS = 8
NR = 2048
NC = 4096
NBR = 16
NBC = 32
REGIONS = 128


def with_ends(array, key, smallest, largest):
    place = [jax.random.randint(jax.random.fold_in(key, axis), (), 0, length) for axis, length in enumerate(array.shape)]
    longest = array.shape.index(max(array.shape))
    neighbour = place[:longest] + [(place[longest] + 1) % array.shape[longest]] + place[longest + 1:]
    return array.at[tuple(place)].set(smallest).at[tuple(neighbour)].set(largest)


def shard_levels(key, dims, split, low, high):
    def one(axis_at, shards_of):
        steps = jax.random.uniform(jax.random.fold_in(jax.random.fold_in(key, 6), axis_at), (shards_of,), jnp.float32, low / len(split), high / len(split))
        return jnp.repeat(jnp.exp(steps), dims[axis_at] // shards_of).reshape((-1,) + (1,) * (len(dims) - axis_at - 1))

    gain = one(*split[0])
    for cut in split[1:]:
        gain = gain * one(*cut)
    return gain


def cumulative_ranks(number_of, skew):
    portions = [(1 << 20) // math.isqrt(rank ** skew) + 1 for rank in range(1, number_of + 1)]
    scale = 1 + sum(portions) // (1 << 30)
    return np.cumsum(np.array([max(1, weight // scale) for weight in portions]))


def skewed_ids(rng, shape, count, skew):
    table = cumulative_ranks(count, skew)
    lot = jax.random.randint(jax.random.fold_in(rng, 1), shape, 0, int(table[count - 1]))
    rank = jnp.searchsorted(jnp.asarray(table, jnp.int32), lot, side="right")
    return jax.random.permutation(jax.random.fold_in(rng, 2), count)[rank].astype(jnp.int32)


def centred(key, dims, scale, most, shards=(), kind=jnp.bfloat16):
    gain = shard_levels(key, dims, shards, -0.22, 0.18) if shards else 1.0
    drawn = jax.random.normal(key, dims, jnp.float32) * scale * gain
    return jnp.minimum(jnp.maximum(drawn, -most), most).astype(kind)


def setup_inputs(seed: int = 0) -> dict:
    key_list = jax.random.split(jax.random.key(seed), 11)
    height = centred(key_list[0], (NR, NC), 1.0, 6.0, ((0, 16), (1, 32)), jnp.float32)
    density = jnp.clip(0.2 + 0.8 * jax.random.uniform(key_list[1], (NR, NC), jnp.float32) ** shard_levels(key_list[1], (NR, NC), ((0, 16), (1, 32)), -0.2, 0.2), 0.2, 1.0)
    target = centred(key_list[2], (NR, NC), 1.0, 6.0, ((0, 16), (1, 32)), jnp.float32)
    region_of_block = with_ends(skewed_ids(key_list[3], (NBR, NBC), REGIONS, 2), jax.random.fold_in(key_list[3], 3), 0, REGIONS - 1).astype(jnp.int32)
    class_of_block = with_ends(jax.random.randint(key_list[4], (NBR, NBC), 0, NCLASS), jax.random.fold_in(key_list[4], 1), 0, NCLASS - 1).astype(jnp.int32)
    fill_level = jnp.clip(jax.random.uniform(key_list[5], (REGIONS,), jnp.float32, 0.0, 0.5), 0.0, 0.5)
    rates = jnp.clip(jnp.exp(jax.random.uniform(key_list[6], (NCLASS,), jnp.float32, math.log(0.1), math.log(0.6))), 0.1, 0.6)
    col_taps = centred(key_list[7], (CHANNELS, TAPS), TAPS ** -0.5, 1.0, (), jnp.float32)
    row_taps = centred(key_list[8], (CHANNELS, TAPS), TAPS ** -0.5, 1.0, (), jnp.float32)
    gains = jnp.clip(jnp.exp(jax.random.uniform(key_list[9], (CHANNELS,), jnp.float32, math.log(0.2), math.log(0.6))), 0.2, 0.6)
    return dict(height=height, density=density, target=target, region_of_block=region_of_block, class_of_block=class_of_block, fill_level=fill_level, rates=rates, col_taps=col_taps, row_taps=row_taps, gains=gains)


def kernel_vectors(tap_weights, length):
    positions = jnp.arange(length, dtype=jnp.int32)
    channel_rows = []
    for channel in range(CHANNELS):
        summed = jnp.zeros((length,), jnp.float32)
        for position in range(TAPS):
            offset = ((position - TAPS // 2) * 2 ** channel) % length
            summed = summed + jnp.where(positions == offset, tap_weights[channel, position], 0.0)
        channel_rows.append(summed)
    rounded = lax.optimization_barrier(jnp.stack(channel_rows).astype(jnp.bfloat16))
    return rounded.astype(jnp.float32)


def circular(grid_values, kernel, axis, transpose):
    length = grid_values.shape[axis]
    spectrum = jnp.fft.rfft(grid_values, axis=axis)
    kernel_spec = jnp.fft.rfft(kernel)
    if transpose:
        kernel_spec = jnp.conj(kernel_spec)
    broadcast_shape = [1, 1]
    broadcast_shape[axis] = kernel_spec.shape[0]
    return jnp.fft.irfft(spectrum * kernel_spec.reshape(broadcast_shape), n=length, axis=axis).astype(jnp.float32)


def to_bf16_back(values):
    return lax.optimization_barrier(values.astype(jnp.bfloat16)).astype(jnp.float32)


def reference(height, density, target, region_of_block, class_of_block, fill_level, rates, col_taps, row_taps, gains):
    total_rows, total_cols = height.shape
    region_hot = (region_of_block[:, :, None] == jnp.arange(fill_level.shape[0], dtype=jnp.int32)).astype(jnp.float32)
    class_hot = (class_of_block[:, :, None] == jnp.arange(rates.shape[0], dtype=jnp.int32)).astype(jnp.float32)
    fill_block = jnp.sum(region_hot * fill_level, axis=2)
    rate_block = jnp.sum(class_hot * rates, axis=2)

    def to_cells(values):
        return jnp.repeat(jnp.repeat(values, BLOCK, axis=0), BLOCK, axis=1)

    effective = density + to_cells(fill_block)
    rate_cells = to_cells(rate_block)
    source = to_bf16_back(effective * height)
    col_kernel = kernel_vectors(col_taps, total_cols)
    row_kernel = kernel_vectors(row_taps, total_rows)
    smoothed = []
    pressure_arg = jnp.zeros((total_rows, total_cols), jnp.float32)
    for channel in range(CHANNELS):
        channel_values = to_bf16_back(circular(source, col_kernel[channel], 1, False))
        smoothed.append(channel_values)
        pressure_arg = pressure_arg + gains[channel] * circular(channel_values, row_kernel[channel], 0, False)
    shifted = 1.0 + pressure_arg
    new_height = height - rate_cells * jax.nn.softplus(shifted)
    pressure_adjoint = to_bf16_back(-(new_height - target) * rate_cells * jax.nn.sigmoid(shifted) / BLOCK)
    source_adjoint = jnp.zeros((total_rows, total_cols), jnp.float32)
    gain_terms = []
    for channel in range(CHANNELS):
        channel_adjoint = circular(pressure_adjoint, row_kernel[channel], 0, True)
        gain_terms.append(jnp.sum(channel_adjoint * smoothed[channel]))
        weighted = to_bf16_back(gains[channel] * channel_adjoint)
        source_adjoint = source_adjoint + circular(weighted, col_kernel[channel], 1, True)
    gain_grad = jnp.stack(gain_terms)
    block_rows, block_cols = region_of_block.shape
    block_sums = jnp.sum((source_adjoint * height).reshape(block_rows, BLOCK, block_cols, BLOCK), axis=(1, 3))
    fill_grad = jnp.sum(region_hot * block_sums[:, :, None], axis=(0, 1))
    return new_height, gain_grad, fill_grad
```

```python
import jax
import jax.numpy as jnp
from jax import lax
from jax.experimental import pallas as pl
from jax.experimental.pallas import tpu as pltpu
from jax.sharding import PartitionSpec as P

CHANNELS = 8
TAPS = 33
HALF = TAPS // 2
SIDE = 128
ROWS = 16
COLS = 32
PEERS = COLS // 2
SUB = SIDE // ROWS
MIXED = CHANNELS - 1
F32 = jnp.float32
BF16 = jnp.bfloat16
VMEM = pl.BlockSpec(memory_space=pltpu.VMEM)
SMEM = pl.BlockSpec(memory_space=pltpu.SMEM)
ANY = pl.BlockSpec(memory_space=pl.ANY)
PARAMS = pltpu.CompilerParams(vmem_limit_bytes=24 * 1024 * 1024)


def reach(channel):
    return max(1, 2**channel * HALF // SIDE)


def blocks(channel):
    return 2 * reach(channel) + 1


def split(values):
    high = values.astype(BF16)
    low = (values - high.astype(F32)).astype(BF16)
    return high, low


def pair_rows(first, second):
    return jnp.concatenate(
        [first.reshape(ROWS, SUB, SIDE), second.reshape(ROWS, SUB, SIDE)], axis=1
    )


def unpair_rows(pairs):
    values = pairs.astype(F32)
    return (
        values[:, :SUB, :].reshape(SIDE, SIDE),
        values[:, SUB:, :].reshape(SIDE, SIDE),
    )


def source_kernel(region_ref, fill_ref, height_ref, density_ref, out_ref):
    fill = fill_ref[region_ref[0, 0]]
    source = (density_ref[...] + fill) * height_ref[...]
    turned = source.T.astype(BF16)
    for peer in range(PEERS):
        out_ref[peer] = turned


def toeplitz(taps_ref, channel, direction, merged):
    width = (blocks(channel) + 1) * SIDE
    lane = lax.broadcasted_iota(jnp.int32, (1, SIDE), 1)
    parts = [jnp.zeros((1, SIDE), F32) for _ in range(width // SIDE)]
    for position in range(TAPS):
        value = taps_ref[channel, position]
        if merged and position == 0:
            continue
        if merged and position == TAPS - 1:
            value = value + taps_ref[channel, 0]
        place = reach(channel) * SIDE + direction * (position - HALF) * 2**channel
        part, inside = divmod(place, SIDE)
        parts[part] = jnp.where(lane == inside, value, parts[part])
    base = jnp.concatenate(parts, axis=1).astype(BF16).astype(F32)
    spread = jnp.broadcast_to(base, (SIDE, width))
    rolled = pltpu.roll(spread, 0, 1, stride=1, stride_axis=0)
    return rolled[:, : blocks(channel) * SIDE].astype(BF16)


def tables_kernel(
    col_ref, row_ref, class_ref, height_ref, target_ref, gathered_ref, *out_refs
):
    col_out, row_out = out_refs[:MIXED], out_refs[MIXED : 2 * MIXED]
    col_last, row_last, extra_ref = out_refs[2 * MIXED :]
    for channel in range(MIXED):
        col_out[channel][...] = toeplitz(col_ref, channel, -1, False)
        row_out[channel][...] = toeplitz(row_ref, channel, 1, channel == 6)
    for step in range(COLS):
        value = col_ref[MIXED, TAPS - 1 - step]
        if step == 0:
            value = value + col_ref[MIXED, 0]
        col_last[step] = jnp.full((SUB, SIDE), value, F32).astype(BF16).astype(F32)
    for step in range(ROWS):
        value = row_ref[MIXED, step] + row_ref[MIXED, step + ROWS]
        if step == 0:
            value = value + row_ref[MIXED, TAPS - 1]
        row_last[step] = jnp.full((SUB, SIDE), value, F32).astype(BF16).astype(F32)
    away = (height_ref[...] - target_ref[...]).T
    high, low = split(away)
    extra_ref[:, :16, :] = pair_rows(high.astype(F32), low.astype(F32)).astype(BF16)
    kind = class_ref[0, 0].astype(F32)
    extra_ref[:, 16:, :] = jnp.full((ROWS, 16, SIDE), kind, F32).astype(BF16)


def smooth_kernel(col_index_ref, own_ref, other_ref, last_ref, extra_ref, *refs):
    tables, out_ref, window_ref = refs[:MIXED], refs[MIXED], refs[MIXED + 1]
    here = col_index_ref[0]
    last = jnp.zeros((SIDE, SIDE), F32)
    for step in range(COLS):
        block = lax.rem(here + (COLS - HALF + step), COLS) // 2
        values = (own_ref if step % 2 == 0 else other_ref)[block]
        window_ref[step * SIDE : (step + 1) * SIDE, :] = values
        scaled = values.astype(F32).reshape(ROWS, SUB, SIDE) * last_ref[step]
        last = last + scaled.reshape(SIDE, SIDE)
    smoothed = []
    for channel in range(MIXED):
        first = (HALF - reach(channel)) * SIDE
        smoothed.append(
            jnp.dot(
                tables[channel][...],
                window_ref[first : first + blocks(channel) * SIDE, :],
                preferred_element_type=F32,
            )
        )
    smoothed.append(last)
    for pair in range(CHANNELS // 2):
        out_ref[:, 16 * pair : 16 * pair + 16, :] = pair_rows(
            smoothed[2 * pair], smoothed[2 * pair + 1]
        ).astype(BF16)
    out_ref[:, 64:, :] = extra_ref[...]


def rolled_rows(values, block_shift):
    shift = block_shift * SUB % SIDE
    if shift == 0:
        return values
    return jnp.concatenate([values[SIDE - shift :], values[: SIDE - shift]], axis=0)


def pressure_kernel(gains_ref, rates_ref, long_ref, last_ref, *refs):
    tables, out_ref, gain_ref = refs[:MIXED], refs[MIXED], refs[MIXED + 1]
    smoothed = []
    for pair in range(CHANNELS // 2):
        smoothed.extend(unpair_rows(long_ref[:, 16 * pair : 16 * pair + 16, :]))
    high, low = unpair_rows(long_ref[:, 64:80, :])
    away = high + low
    kind, _ = unpair_rows(long_ref[:, 80:96, :])
    rate = jnp.zeros((SIDE, SIDE), F32)
    for number in range(rates_ref.shape[0]):
        rate = jnp.where(kind == float(number), rates_ref[number], rate)

    pressure = jnp.zeros((SIDE, SIDE), F32)
    for channel in range(MIXED):
        spread = jnp.dot(
            smoothed[channel].astype(BF16), tables[channel][...], preferred_element_type=F32
        )
        total = None
        for block in range(blocks(channel)):
            term = rolled_rows(
                spread[:, block * SIDE : (block + 1) * SIDE], block - reach(channel)
            )
            total = term if total is None else total + term
        pressure = pressure + gains_ref[channel] * total
    total = jnp.zeros((SIDE, SIDE), F32)
    for step in range(ROWS):
        scaled = smoothed[MIXED].reshape(ROWS, SUB, SIDE) * last_ref[step]
        total = total + rolled_rows(scaled.reshape(SIDE, SIDE), step)
    pressure = pressure + gains_ref[MIXED] * total

    shifted = 1.0 + pressure
    decay = jnp.exp(-jnp.abs(shifted))
    removed = rate * (jnp.maximum(shifted, 0.0) + jnp.log1p(decay))
    slope = jnp.where(shifted >= 0, 1.0, decay) / (1.0 + decay)
    adjoint = (-(away - removed) * rate * slope / SIDE).astype(BF16)

    weighted = []
    gain_rows = []
    for channel in range(CHANNELS):
        total = jnp.zeros((SIDE, SIDE), F32)
        if channel < MIXED:
            for block in range(blocks(channel)):
                term = lax.dot_general(
                    adjoint,
                    tables[channel][:, block * SIDE : (block + 1) * SIDE],
                    (((1,), (1,)), ((), ())),
                    preferred_element_type=F32,
                )
                total = total + rolled_rows(term, reach(channel) - block)
        else:
            wide = adjoint.astype(F32).reshape(ROWS, SUB, SIDE)
            for step in range(ROWS):
                scaled = wide * last_ref[step]
                total = total + rolled_rows(scaled.reshape(SIDE, SIDE), -step)
        gain_rows.append(jnp.sum(total * smoothed[channel], axis=0, keepdims=True))
        weighted.append(gains_ref[channel] * total)
    for pair in range(CHANNELS // 2):
        out_ref[:, 16 * pair : 16 * pair + 16, :] = pair_rows(
            weighted[2 * pair], weighted[2 * pair + 1]
        ).astype(BF16)
    high, low = split(removed)
    out_ref[:, 64:, :] = pair_rows(high.astype(F32), low.astype(F32)).astype(BF16)
    gain_ref[...] = jnp.concatenate(gain_rows, axis=0)


def gradient_kernel(
    col_index_ref, back_ref, band_ref, last_ref, gain_ref, height_ref, *refs
):
    tables, new_ref, sums_ref = refs[:MIXED], refs[MIXED], refs[MIXED + 1]
    here = col_index_ref[0]
    weighted = []
    for pair in range(CHANNELS // 2):
        weighted.extend(unpair_rows(back_ref[:, 16 * pair : 16 * pair + 16, :]))
    high, low = unpair_rows(back_ref[:, 64:80, :])
    new_ref[...] = height_ref[...] - (high + low).T
    turned = weighted[MIXED].T
    doubled = []
    for channel in range(MIXED):
        narrow = weighted[channel].astype(BF16)
        doubled.append(jnp.concatenate([narrow, narrow], axis=1))
    lane = lax.broadcasted_iota(jnp.int32, (SUB, SIDE), 1)
    fill = jnp.zeros((SUB, SIDE), F32)
    for step in range(COLS):
        block = lax.rem(here + (COLS - HALF + step), COLS)
        values = band_ref[block, :SIDE, :]
        region = band_ref[block, SIDE:, :]
        product = jnp.sum((turned * values).reshape(ROWS, SUB, SIDE), axis=0)
        terms = product * last_ref[step]
        ahead = step - HALF
        channels = [c for c in range(MIXED) if abs(ahead) <= reach(c)]
        if channels:
            both = jnp.concatenate(split(values), axis=0)
            for channel in channels:
                place = (ahead + reach(channel)) * SIDE
                cross = jnp.dot(doubled[channel], both, preferred_element_type=F32)
                taps = tables[channel][:, place : place + SIDE].astype(F32)
                terms = terms + jnp.sum((cross * taps).reshape(ROWS, SUB, SIDE), axis=0)
        total = jnp.sum(terms, axis=1, keepdims=True)
        fill = fill + jnp.where(region == lane.astype(F32), total, 0.0)
    gain = jnp.sum(gain_ref[...], axis=1, keepdims=True)
    row = lax.broadcasted_iota(jnp.int32, (SUB, SIDE), 0)
    gain = jnp.where(row == lane, gain, 0.0)
    fill_row = jnp.sum(fill, axis=0, keepdims=True)
    gain_row = jnp.sum(gain, axis=0, keepdims=True)
    both = jnp.concatenate([fill_row, gain_row], axis=0)
    for peer in range(COLS):
        sums_ref[peer] = both


def shape(*dims, dtype=F32):
    return jax.ShapeDtypeStruct(dims, dtype)


def shards(
    height,
    density,
    target,
    region_of_block,
    class_of_block,
    fill_level,
    rates,
    col_taps,
    row_taps,
    gains,
):
    col_index = lax.axis_index("col").astype(jnp.int32).reshape(1)
    marks = jnp.broadcast_to(region_of_block.astype(F32), (SUB, SIDE))
    marked = jnp.concatenate([height, marks], axis=0)
    band = lax.all_gather(marked, "col", axis=0, tiled=False)

    copies = pl.pallas_call(
        source_kernel,
        out_shape=shape(PEERS, SIDE, SIDE, dtype=BF16),
        in_specs=[SMEM, SMEM, VMEM, VMEM],
        out_specs=VMEM,
        compiler_params=PARAMS,
        name="source",
    )(region_of_block, fill_level, height, density)
    groups = [[2 * block + core for block in range(PEERS)] for core in range(2)]
    own = lax.all_to_all(copies, "col", 0, 0, axis_index_groups=groups, tiled=True)
    other = lax.ppermute(own, "col", [(block, block ^ 1) for block in range(COLS)])

    table_shapes = [shape(SIDE, blocks(c) * SIDE, dtype=BF16) for c in range(MIXED)]
    made = pl.pallas_call(
        tables_kernel,
        out_shape=table_shapes
        + table_shapes
        + [shape(COLS, SUB, SIDE), shape(ROWS, SUB, SIDE), shape(ROWS, 32, SIDE, dtype=BF16)],
        in_specs=[SMEM, SMEM, SMEM, VMEM, VMEM, ANY],
        out_specs=[VMEM] * (2 * MIXED + 3),
        compiler_params=PARAMS,
        cost_estimate=pl.CostEstimate(flops=4000000, bytes_accessed=4000000, transcendentals=0),
        name="tables",
    )(col_taps, row_taps, class_of_block, height, target, own)
    col_tables, row_tables = made[:MIXED], made[MIXED : 2 * MIXED]
    col_last, row_last, extra = made[2 * MIXED :]

    smoothed = pl.pallas_call(
        smooth_kernel,
        out_shape=shape(ROWS, 96, SIDE, dtype=BF16),
        in_specs=[SMEM] + [VMEM] * (4 + MIXED),
        out_specs=VMEM,
        scratch_shapes=[pltpu.VMEM((COLS * SIDE, SIDE), BF16)],
        compiler_params=PARAMS,
        name="smooth",
    )(col_index, own, other, col_last, extra, *col_tables)
    long = lax.all_to_all(smoothed, "row", 0, 0, tiled=True)

    back, gain_part = pl.pallas_call(
        pressure_kernel,
        out_shape=[shape(ROWS, 80, SIDE, dtype=BF16), shape(CHANNELS, SIDE)],
        in_specs=[SMEM, SMEM] + [VMEM] * (2 + MIXED),
        out_specs=[VMEM, VMEM],
        compiler_params=PARAMS,
        name="pressure",
    )(gains, rates, long, row_last, *row_tables)
    tile = lax.all_to_all(back, "row", 0, 0, tiled=True)

    new_height, sums = pl.pallas_call(
        gradient_kernel,
        out_shape=[shape(SIDE, SIDE), shape(COLS, 2, SIDE)],
        in_specs=[SMEM] + [VMEM] * (5 + MIXED),
        out_specs=[VMEM, VMEM],
        compiler_params=PARAMS,
        name="gradient",
    )(col_index, tile, band, col_last, gain_part, height, *col_tables)
    by_col = lax.all_to_all(sums, "col", 0, 0, tiled=True)
    band_sum = jnp.sum(by_col, axis=0, keepdims=True)
    by_row = lax.all_to_all(
        jnp.broadcast_to(band_sum, (ROWS, 2, SIDE)), "row", 0, 0, tiled=True
    )
    total = jnp.sum(by_row, axis=0)
    return new_height, total[1, :CHANNELS], total[0]


def solution(mesh):
    cells = P("row", "col")
    in_specs = (cells,) * 5 + (P(),) * 5
    out_specs = (cells, P(), P())
    return jax.shard_map(shards, mesh=mesh, in_specs=in_specs, out_specs=out_specs, check_vma=False)
```

```python
import functools

import jax
import jax.numpy as jnp
from jax import lax
from jax.experimental import pallas as pl
from jax.experimental.pallas import tpu as pltpu
from jax.sharding import PartitionSpec as P

CHANNELS = 8
TAPS = 33
HALF = TAPS // 2
SIDE = 128
ROWS = 16
COLS = 32
PEERS = COLS // 2
SUB = SIDE // ROWS
MIXED = CHANNELS - 1
F32 = jnp.float32
BF16 = jnp.bfloat16
VMEM = pl.BlockSpec(memory_space=pltpu.VMEM)
SMEM = pl.BlockSpec(memory_space=pltpu.SMEM)
ANY = pl.BlockSpec(memory_space=pl.ANY)
HBM = pl.BlockSpec(memory_space=pltpu.HBM)
PARAMS = pltpu.CompilerParams(vmem_limit_bytes=24 * 1024 * 1024)


def reach(channel):
    return max(1, 2**channel * HALF // SIDE)


def blocks(channel):
    return 2 * reach(channel) + 1


def split(values):
    high = values.astype(BF16)
    low = (values - high.astype(F32)).astype(BF16)
    return high, low


def pair_rows(first, second):
    return jnp.concatenate(
        [first.reshape(ROWS, SUB, SIDE), second.reshape(ROWS, SUB, SIDE)], axis=1
    )


def unpair_rows(pairs):
    values = pairs.astype(F32)
    return (
        values[:, :SUB, :].reshape(SIDE, SIDE),
        values[:, SUB:, :].reshape(SIDE, SIDE),
    )


def scaled(values, scale):
    return (values.reshape(ROWS, SUB, SIDE) * scale).reshape(SIDE, SIDE)


def fetch(sources, targets, sem):
    copies = [
        pltpu.make_async_copy(source, target, sem.at[number])
        for number, (source, target) in enumerate(zip(sources, targets))
    ]
    for copy in copies:
        copy.start()
    for copy in copies:
        copy.wait()


def scatter_round(values, place):
    near = values.astype(BF16).astype(F32)
    step = (near * (1.0 + 0.7 / 128)).astype(BF16).astype(F32) - near
    row = lax.broadcasted_iota(jnp.int32, values.shape, 0).astype(F32)
    column = lax.broadcasted_iota(jnp.int32, values.shape, 1).astype(F32)
    mixed = row * 0.7548777 + column * 0.5698403 + place.astype(F32) * 0.6180340
    return (values + step * (mixed - jnp.floor(mixed) - 0.5)).astype(BF16)


def source_kernel(place_ref, region_ref, fill_in, height_in, density_in, out_ref, *scratch):
    fill_ref, height_ref, density_ref, sem = scratch
    fetch((fill_in, height_in, density_in), (fill_ref, height_ref, density_ref), sem)
    fill = fill_ref[region_ref[0, 0]]
    height = height_ref[...]
    source = (density_ref[...] + fill) * height
    turned = source.T.astype(BF16)
    rounded = scatter_round(height, place_ref[0])
    for peer in range(PEERS):
        out_ref[peer, :SIDE, :] = turned
        out_ref[peer, SIDE:, :] = rounded


def toeplitz(taps_ref, channel, direction, merged):
    width = (blocks(channel) + 1) * SIDE
    lane = lax.broadcasted_iota(jnp.int32, (1, SIDE), 1)
    parts = [jnp.zeros((1, SIDE), F32) for _ in range(width // SIDE)]
    for position in range(TAPS):
        value = taps_ref[channel, position]
        if merged and position == 0:
            continue
        if merged and position == TAPS - 1:
            value = value + taps_ref[channel, 0]
        place = reach(channel) * SIDE + direction * (position - HALF) * 2**channel
        part, inside = divmod(place, SIDE)
        parts[part] = jnp.where(lane == inside, value, parts[part])
    base = jnp.concatenate(parts, axis=1).astype(BF16).astype(F32)
    spread = jnp.broadcast_to(base, (SIDE, width))
    rolled = pltpu.roll(spread, 0, 1, stride=1, stride_axis=0)
    return rolled[:, : blocks(channel) * SIDE].astype(BF16)


def fill_tables(taps_ref, outs, last_ref, direction, merged):
    for channel in range(MIXED):
        outs[channel][...] = toeplitz(taps_ref, channel, direction, merged and channel == 6)
    steps = last_ref.shape[0]
    for step in range(steps):
        places = [t for t in range(TAPS) if (direction * (t - HALF) + HALF - step) % steps == 0]
        value = taps_ref[MIXED, places[0]]
        for place in places[1:]:
            value = value + taps_ref[MIXED, place]
        last_ref[step] = jnp.full((SUB, SIDE), value, F32).astype(BF16).astype(F32)


def tables_kernel(col_in, row_in, gains_in, rates_in, after_ref, *refs):
    scales_ref, col_ref, row_ref, gains_ref, rates_ref, sem = refs[2 * MIXED + 2 :]
    fetch(
        (col_in, row_in, gains_in, rates_in), (col_ref, row_ref, gains_ref, rates_ref), sem
    )
    for number in range(CHANNELS):
        scales_ref[number] = jnp.full((SUB, SIDE), gains_ref[number], F32)
        scales_ref[CHANNELS + number] = jnp.full((SUB, SIDE), rates_ref[number], F32)
    fill_tables(col_ref, refs[:MIXED], refs[MIXED], -1, False)
    fill_tables(row_ref, refs[MIXED + 1 : 2 * MIXED + 1], refs[2 * MIXED + 1], 1, True)


def smooth_kernel(place_ref, class_ref, own_ref, other_ref, height_in, target_in, last_ref, *refs):
    tables, out_ref = refs[:MIXED], refs[MIXED]
    window_ref, height_ref, target_ref, sem = refs[MIXED + 1 :]
    copies = [
        pltpu.make_async_copy(height_in, height_ref, sem.at[0]),
        pltpu.make_async_copy(target_in, target_ref, sem.at[1]),
    ]
    for copy in copies:
        copy.start()
    here = place_ref[0]
    last = jnp.zeros((SIDE, SIDE), F32)
    for step in range(COLS):
        block = lax.rem(here + (COLS - HALF + step), COLS) // 2
        chunk_ref = own_ref if step % 2 == 0 else other_ref
        values = chunk_ref[block, :SIDE, :]
        window_ref[step * SIDE : (step + 1) * SIDE, :] = values
        last = last + scaled(values.astype(F32), last_ref[step])
    smoothed = []
    for channel in range(MIXED):
        first = (HALF - reach(channel)) * SIDE
        smoothed.append(
            jnp.dot(
                tables[channel][...],
                window_ref[first : first + blocks(channel) * SIDE, :],
                preferred_element_type=F32,
            )
        )
    smoothed.append(last)
    for pair in range(CHANNELS // 2):
        out_ref[:, 16 * pair : 16 * pair + 16, :] = pair_rows(
            smoothed[2 * pair], smoothed[2 * pair + 1]
        ).astype(BF16)
    for copy in copies:
        copy.wait()
    away = (height_ref[...] - target_ref[...]).T
    high, low = split(away)
    out_ref[:, 64:80, :] = pair_rows(high.astype(F32), low.astype(F32)).astype(BF16)
    kind = class_ref[0, 0].astype(F32)
    out_ref[:, 80:, :] = jnp.full((ROWS, 16, SIDE), kind, F32).astype(BF16)


def rolled_rows(values, block_shift):
    shift = block_shift * SUB % SIDE
    if shift == 0:
        return values
    return jnp.concatenate([values[SIDE - shift :], values[: SIDE - shift]], axis=0)


def pressure_kernel(scales_ref, long_ref, last_ref, *refs):
    tables, out_ref, gain_ref = refs[:MIXED], refs[MIXED], refs[MIXED + 1]
    smoothed = []
    for pair in range(CHANNELS // 2):
        smoothed.extend(unpair_rows(long_ref[:, 16 * pair : 16 * pair + 16, :]))
    high, low = unpair_rows(long_ref[:, 64:80, :])
    away = high + low
    kind, _ = unpair_rows(long_ref[:, 80:96, :])
    kind = kind.reshape(ROWS, SUB, SIDE)
    rate = jnp.zeros((ROWS, SUB, SIDE), F32)
    for number in range(CHANNELS):
        rate = jnp.where(kind == float(number), scales_ref[CHANNELS + number], rate)
    rate = rate.reshape(SIDE, SIDE)

    pressure = jnp.zeros((SIDE, SIDE), F32)
    for channel in range(MIXED):
        spread = jnp.dot(
            smoothed[channel].astype(BF16), tables[channel][...], preferred_element_type=F32
        )
        total = None
        for block in range(blocks(channel)):
            term = rolled_rows(
                spread[:, block * SIDE : (block + 1) * SIDE], block - reach(channel)
            )
            total = term if total is None else total + term
        pressure = pressure + scaled(total, scales_ref[channel])
    total = jnp.zeros((SIDE, SIDE), F32)
    for step in range(ROWS):
        total = total + rolled_rows(scaled(smoothed[MIXED], last_ref[step]), step)
    pressure = pressure + scaled(total, scales_ref[MIXED])

    shifted = 1.0 + pressure
    decay = jnp.exp(-jnp.abs(shifted))
    removed = rate * (jnp.maximum(shifted, 0.0) + jnp.log1p(decay))
    slope = jnp.where(shifted >= 0, 1.0, decay) / (1.0 + decay)
    adjoint = (-(away - removed) * rate * slope / SIDE).astype(BF16)

    weighted = []
    gain_rows = []
    for channel in range(CHANNELS):
        total = jnp.zeros((SIDE, SIDE), F32)
        if channel < MIXED:
            for block in range(blocks(channel)):
                term = lax.dot_general(
                    adjoint,
                    tables[channel][:, block * SIDE : (block + 1) * SIDE],
                    (((1,), (1,)), ((), ())),
                    preferred_element_type=F32,
                )
                total = total + rolled_rows(term, reach(channel) - block)
        else:
            wide = adjoint.astype(F32)
            for step in range(ROWS):
                total = total + rolled_rows(scaled(wide, last_ref[step]), -step)
        gain_rows.append(jnp.sum(total * smoothed[channel], axis=0, keepdims=True))
        weighted.append(scaled(total, scales_ref[channel]))
    for pair in range(CHANNELS // 2):
        out_ref[:, 16 * pair : 16 * pair + 16, :] = pair_rows(
            weighted[2 * pair], weighted[2 * pair + 1]
        ).astype(BF16)
    high, low = split(removed)
    out_ref[:, 64:, :] = pair_rows(high.astype(F32), low.astype(F32)).astype(BF16)
    gain_ref[...] = jnp.concatenate(gain_rows, axis=0)


def gradient_kernel(
    place_ref, region_ref, back_ref, own_ref, other_ref, gain_ref, height_in, last_ref, *refs
):
    tables, new_ref, sums_ref = refs[:MIXED], refs[MIXED], refs[MIXED + 1]
    height_ref, sem = refs[MIXED + 2 :]
    copy = pltpu.make_async_copy(height_in, height_ref, sem.at[0])
    copy.start()
    weighted = []
    for pair in range(CHANNELS // 2):
        weighted.extend(unpair_rows(back_ref[:, 16 * pair : 16 * pair + 16, :]))
    turned = weighted[MIXED].T
    narrow = [weighted[channel].astype(BF16) for channel in range(MIXED)]
    here = place_ref[0]
    lane = lax.broadcasted_iota(jnp.int32, (1, SIDE), 1)
    line = jnp.zeros((1, SIDE), F32)
    for step in range(COLS):
        block = lax.rem(here + (COLS - HALF + step), COLS) // 2
        values = (own_ref if step % 2 == 0 else other_ref)[block, SIDE:, :]
        product = turned * values.astype(F32)
        product = jnp.sum(product.reshape(ROWS, SUB, SIDE), axis=0)
        terms = product * last_ref[step]
        ahead = step - HALF
        channels = [c for c in range(MIXED) if abs(ahead) <= reach(c)]
        for channel in channels:
            first = (ahead + reach(channel)) * SIDE
            cross = jnp.dot(narrow[channel], values, preferred_element_type=F32)
            taps = tables[channel][:, first : first + SIDE].astype(F32)
            terms = terms + jnp.sum((cross * taps).reshape(ROWS, SUB, SIDE), axis=0)
        total = jnp.sum(jnp.sum(terms, axis=0, keepdims=True), axis=1, keepdims=True)
        line = line + jnp.where(lane == step, total, 0.0)
    gain = jnp.sum(gain_ref[...], axis=1, keepdims=True)
    row = lax.broadcasted_iota(jnp.int32, (SUB, SIDE), 0)
    wide_lane = lax.broadcasted_iota(jnp.int32, (SUB, SIDE), 1)
    gain = jnp.sum(jnp.where(row + COLS == wide_lane, gain, 0.0), axis=0, keepdims=True)
    region = region_ref[0, 0].astype(F32)
    line = line + gain + jnp.where(lane == COLS + SUB, region, 0.0)
    for peer in range(COLS):
        sums_ref[peer] = line
    high, low = unpair_rows(back_ref[:, 64:80, :])
    copy.wait()
    new_ref[...] = height_ref[...] - (high + low).T


def regions_kernel(place_ref, lines_ref, out_ref):
    lines = lines_ref[...].reshape(COLS, SIDE)
    sender = lax.broadcasted_iota(jnp.int32, (COLS, SIDE), 0)
    lane = lax.broadcasted_iota(jnp.int32, (COLS, SIDE), 1)
    sums = jnp.where(lane < COLS, lines, 0.0)
    region = jnp.sum(jnp.where(lane == COLS + SUB, lines, 0.0), axis=1, keepdims=True)
    gain = jnp.sum(jnp.where((lane >= COLS) & (lane < COLS + SUB), lines, 0.0), axis=0, keepdims=True)
    fill = jnp.zeros((1, SIDE), F32)
    for block in range(COLS):
        held = jnp.sum(jnp.where(lane == lax.rem(block + HALF - sender + COLS, COLS), sums, 0.0))
        fill = fill + jnp.where(region[block : block + 1] == lane[:1].astype(F32), held, 0.0)
    both = jnp.concatenate([fill, gain], axis=0)
    for peer in range(ROWS):
        out_ref[peer] = both


def total_kernel(sums_ref, fill_ref, gain_ref):
    total = jnp.sum(sums_ref[...], axis=0)
    fill_ref[...] = total[0]
    gain_ref[...] = total[1, COLS : COLS + CHANNELS]


def shape(*dims, dtype=F32):
    return jax.ShapeDtypeStruct(dims, dtype)


def shards(
    height,
    density,
    target,
    region_of_block,
    class_of_block,
    fill_level,
    rates,
    col_taps,
    row_taps,
    gains,
):
    place = lax.axis_index("col").astype(jnp.int32).reshape(1)
    copies = pl.pallas_call(
        source_kernel,
        out_shape=shape(PEERS, 2 * SIDE, SIDE, dtype=BF16),
        in_specs=[SMEM, SMEM, HBM, HBM, HBM],
        out_specs=VMEM,
        scratch_shapes=[
            pltpu.SMEM((SIDE,), F32),
            pltpu.VMEM((SIDE, SIDE), F32),
            pltpu.VMEM((SIDE, SIDE), F32),
            pltpu.SemaphoreType.DMA((3,)),
        ],
        compiler_params=pltpu.CompilerParams(vmem_limit_bytes=60 * 1024 * 1024),
        name="source",
    )(place, region_of_block, fill_level, height, density)
    groups = [[2 * block + core for block in range(PEERS)] for core in range(2)]
    own = lax.all_to_all(copies, "col", 0, 0, axis_index_groups=groups, tiled=True)
    other = lax.ppermute(own, "col", [(block, block ^ 1) for block in range(COLS)])
    table_shapes = [shape(SIDE, blocks(c) * SIDE, dtype=BF16) for c in range(MIXED)]
    made = pl.pallas_call(
        tables_kernel,
        out_shape=table_shapes
        + [shape(COLS, SUB, SIDE)]
        + table_shapes
        + [shape(ROWS, SUB, SIDE), shape(2 * CHANNELS, SUB, SIDE)],
        in_specs=[HBM] * 4 + [ANY],
        out_specs=[VMEM] * (2 * MIXED + 3),
        scratch_shapes=[
            pltpu.SMEM((CHANNELS, TAPS), F32),
            pltpu.SMEM((CHANNELS, TAPS), F32),
            pltpu.SMEM((CHANNELS,), F32),
            pltpu.SMEM((CHANNELS,), F32),
            pltpu.SemaphoreType.DMA((4,)),
        ],
        compiler_params=PARAMS,
        cost_estimate=pl.CostEstimate(flops=4000000, bytes_accessed=4000000, transcendentals=0),
        name="tables",
    )(col_taps, row_taps, gains, rates, own)
    col_tables, col_last = made[:MIXED], made[MIXED]
    row_tables, row_last = made[MIXED + 1 : 2 * MIXED + 1], made[2 * MIXED + 1]
    scales = made[2 * MIXED + 2]

    smoothed = pl.pallas_call(
        smooth_kernel,
        out_shape=shape(ROWS, 96, SIDE, dtype=BF16),
        in_specs=[SMEM, SMEM, VMEM, VMEM, HBM, HBM] + [VMEM] * (1 + MIXED),
        out_specs=VMEM,
        scratch_shapes=[
            pltpu.VMEM((COLS * SIDE, SIDE), BF16),
            pltpu.VMEM((SIDE, SIDE), F32),
            pltpu.VMEM((SIDE, SIDE), F32),
            pltpu.SemaphoreType.DMA((2,)),
        ],
        compiler_params=PARAMS,
        name="smooth",
    )(place, class_of_block, own, other, height, target, col_last, *col_tables)
    long = lax.all_to_all(smoothed, "row", 0, 0, tiled=True)

    back, gain_part = pl.pallas_call(
        pressure_kernel,
        out_shape=[shape(ROWS, 80, SIDE, dtype=BF16), shape(CHANNELS, SIDE)],
        in_specs=[VMEM] * (3 + MIXED),
        out_specs=[VMEM, VMEM],
        compiler_params=PARAMS,
        name="pressure",
    )(scales, long, row_last, *row_tables)
    tile = lax.all_to_all(back, "row", 0, 0, tiled=True)
    new_height, lines = pl.pallas_call(
        gradient_kernel,
        out_shape=[shape(SIDE, SIDE), shape(COLS, 1, SIDE)],
        in_specs=[SMEM, SMEM] + [VMEM] * 4 + [HBM] + [VMEM] * (1 + MIXED),
        out_specs=[VMEM, VMEM],
        scratch_shapes=[pltpu.VMEM((SIDE, SIDE), F32), pltpu.SemaphoreType.DMA((1,))],
        compiler_params=PARAMS,
        name="gradient",
    )(place, region_of_block, tile, own, other, gain_part, height, col_last, *col_tables)
    by_col = lax.all_to_all(lines, "col", 0, 0, tiled=True)
    sums = pl.pallas_call(
        regions_kernel,
        out_shape=shape(ROWS, 2, SIDE),
        in_specs=[SMEM, VMEM],
        out_specs=VMEM,
        compiler_params=PARAMS,
        name="regions",
    )(place, by_col)
    by_row = lax.all_to_all(sums, "row", 0, 0, tiled=True)
    fill_grad, gain_grad = pl.pallas_call(
        total_kernel,
        out_shape=[shape(SIDE), shape(CHANNELS)],
        in_specs=[VMEM],
        out_specs=[VMEM, VMEM],
        compiler_params=PARAMS,
        name="total",
    )(by_row)
    return new_height, gain_grad, fill_grad


def solution(mesh):
    cells = P("row", "col")
    in_specs = (cells,) * 5 + (P(),) * 5
    out_specs = (cells, P(), P())
    return jax.shard_map(shards, mesh=mesh, in_specs=in_specs, out_specs=out_specs, check_vma=False)
```

```python
import functools

import jax
import jax.numpy as jnp
from jax import lax
from jax.experimental import pallas as pl
from jax.experimental.pallas import tpu as pltpu
from jax.sharding import PartitionSpec as P

CHANNELS = 8
TAPS = 33
HALF = TAPS // 2
SIDE = 128
ROWS = 16
COLS = 32
PEERS = COLS // 2
SUB = SIDE // ROWS
MIXED = CHANNELS - 1
F32 = jnp.float32
BF16 = jnp.bfloat16
VMEM = pl.BlockSpec(memory_space=pltpu.VMEM)
SMEM = pl.BlockSpec(memory_space=pltpu.SMEM)
ANY = pl.BlockSpec(memory_space=pl.ANY)
HBM = pl.BlockSpec(memory_space=pltpu.HBM)
PARAMS = pltpu.CompilerParams(vmem_limit_bytes=24 * 1024 * 1024)


def reach(channel):
    return max(1, 2**channel * HALF // SIDE)


def blocks(channel):
    return 2 * reach(channel) + 1


def split(values):
    high = values.astype(BF16)
    low = (values - high.astype(F32)).astype(BF16)
    return high, low


def pair_rows(first, second):
    return jnp.concatenate(
        [first.reshape(ROWS, SUB, SIDE), second.reshape(ROWS, SUB, SIDE)], axis=1
    )


def unpair_rows(pairs):
    values = pairs.astype(F32)
    return (
        values[:, :SUB, :].reshape(SIDE, SIDE),
        values[:, SUB:, :].reshape(SIDE, SIDE),
    )


def scaled(values, scale):
    return (values.reshape(ROWS, SUB, SIDE) * scale).reshape(SIDE, SIDE)


def fetch(sources, targets, sem):
    copies = [
        pltpu.make_async_copy(source, target, sem.at[number])
        for number, (source, target) in enumerate(zip(sources, targets))
    ]
    for copy in copies:
        copy.start()
    for copy in copies:
        copy.wait()


def scatter_round(values, place):
    near = values.astype(BF16).astype(F32)
    step = (near * (1.0 + 0.7 / 128)).astype(BF16).astype(F32) - near
    row = lax.broadcasted_iota(jnp.int32, values.shape, 0).astype(F32)
    column = lax.broadcasted_iota(jnp.int32, values.shape, 1).astype(F32)
    mixed = row * 0.7548777 + column * 0.5698403 + place.astype(F32) * 0.6180340
    return (values + step * (mixed - jnp.floor(mixed) - 0.5)).astype(BF16)


def source_kernel(place_ref, region_ref, fill_in, height_in, density_in, out_ref, *scratch):
    fill_ref, height_ref, density_ref, sem = scratch
    fetch((fill_in, height_in, density_in), (fill_ref, height_ref, density_ref), sem)
    fill = fill_ref[region_ref[0, 0]]
    height = height_ref[...]
    source = (density_ref[...] + fill) * height
    turned = source.T.astype(BF16)
    rounded = scatter_round(height, place_ref[0])
    for peer in range(PEERS):
        out_ref[peer, :SIDE, :] = turned
        out_ref[peer, SIDE:, :] = rounded


def toeplitz(taps_ref, channel, direction, merged):
    width = (blocks(channel) + 1) * SIDE
    lane = lax.broadcasted_iota(jnp.int32, (1, SIDE), 1)
    parts = [jnp.zeros((1, SIDE), F32) for _ in range(width // SIDE)]
    for position in range(TAPS):
        value = taps_ref[channel, position]
        if merged and position == 0:
            continue
        if merged and position == TAPS - 1:
            value = value + taps_ref[channel, 0]
        place = reach(channel) * SIDE + direction * (position - HALF) * 2**channel
        part, inside = divmod(place, SIDE)
        parts[part] = jnp.where(lane == inside, value, parts[part])
    base = jnp.concatenate(parts, axis=1).astype(BF16).astype(F32)
    spread = jnp.broadcast_to(base, (SIDE, width))
    rolled = pltpu.roll(spread, 0, 1, stride=1, stride_axis=0)
    return rolled[:, : blocks(channel) * SIDE].astype(BF16)


def fill_tables(taps_ref, outs, last_ref, direction, merged):
    for channel in range(MIXED):
        outs[channel][...] = toeplitz(taps_ref, channel, direction, merged and channel == 6)
    steps = last_ref.shape[0]
    for step in range(steps):
        places = [t for t in range(TAPS) if (direction * (t - HALF) + HALF - step) % steps == 0]
        value = taps_ref[MIXED, places[0]]
        for place in places[1:]:
            value = value + taps_ref[MIXED, place]
        last_ref[step] = jnp.full((SUB, SIDE), value, F32).astype(BF16).astype(F32)


def tables_kernel(col_in, row_in, gains_in, rates_in, after_ref, *refs):
    scales_ref, col_ref, row_ref, gains_ref, rates_ref, sem = refs[2 * MIXED + 2 :]
    fetch(
        (col_in, row_in, gains_in, rates_in), (col_ref, row_ref, gains_ref, rates_ref), sem
    )
    for number in range(CHANNELS):
        scales_ref[number] = jnp.full((SUB, SIDE), gains_ref[number], F32)
        scales_ref[CHANNELS + number] = jnp.full((SUB, SIDE), rates_ref[number], F32)
    fill_tables(col_ref, refs[:MIXED], refs[MIXED], -1, False)
    fill_tables(row_ref, refs[MIXED + 1 : 2 * MIXED + 1], refs[2 * MIXED + 1], 1, True)


def smooth_kernel(place_ref, class_ref, own_ref, other_ref, height_in, target_in, last_ref, *refs):
    tables, out_ref = refs[:MIXED], refs[MIXED]
    window_ref, height_ref, target_ref, sem = refs[MIXED + 1 :]
    copies = [
        pltpu.make_async_copy(height_in, height_ref, sem.at[0]),
        pltpu.make_async_copy(target_in, target_ref, sem.at[1]),
    ]
    for copy in copies:
        copy.start()
    here = place_ref[0]
    last = jnp.zeros((SIDE, SIDE), F32)
    for step in range(COLS):
        block = lax.rem(here + (COLS - HALF + step), COLS) // 2
        chunk_ref = own_ref if step % 2 == 0 else other_ref
        values = chunk_ref[block, :SIDE, :]
        window_ref[step * SIDE : (step + 1) * SIDE, :] = values
        last = last + scaled(values.astype(F32), last_ref[step])
    smoothed = []
    for channel in range(MIXED):
        first = (HALF - reach(channel)) * SIDE
        smoothed.append(
            jnp.dot(
                tables[channel][...],
                window_ref[first : first + blocks(channel) * SIDE, :],
                preferred_element_type=F32,
            )
        )
    smoothed.append(last)
    for pair in range(CHANNELS // 2):
        out_ref[:, 16 * pair : 16 * pair + 16, :] = pair_rows(
            smoothed[2 * pair], smoothed[2 * pair + 1]
        ).astype(BF16)
    for copy in copies:
        copy.wait()
    away = (height_ref[...] - target_ref[...]).T
    high, low = split(away)
    row = lax.broadcasted_iota(jnp.int32, (SIDE, SIDE), 0)
    lane = lax.broadcasted_iota(jnp.int32, (SIDE, SIDE), 1)
    first = (row % SUB == 0) & (lane == 0)
    low = jnp.where(first, class_ref[0, 0].astype(F32), low.astype(F32))
    out_ref[:, 64:, :] = pair_rows(high.astype(F32), low).astype(BF16)


def rolled_rows(values, block_shift):
    shift = block_shift * SUB % SIDE
    if shift == 0:
        return values
    return jnp.concatenate([values[SIDE - shift :], values[: SIDE - shift]], axis=0)


def pressure_kernel(scales_ref, long_ref, last_ref, *refs):
    tables, out_ref, gain_ref = refs[:MIXED], refs[MIXED], refs[MIXED + 1]
    smoothed = []
    for pair in range(CHANNELS // 2):
        smoothed.extend(unpair_rows(long_ref[:, 16 * pair : 16 * pair + 16, :]))
    high, low = unpair_rows(long_ref[:, 64:, :])
    low = low.reshape(ROWS, SUB, SIDE)
    row = lax.broadcasted_iota(jnp.int32, (ROWS, SUB, SIDE), 1)
    lane = lax.broadcasted_iota(jnp.int32, (ROWS, SUB, SIDE), 2)
    first = (row == 0) & (lane == 0)
    kind = jnp.max(jnp.where(first, low, 0.0), axis=(1, 2), keepdims=True)
    away = high + jnp.where(first, 0.0, low).reshape(SIDE, SIDE)
    rate = jnp.zeros((ROWS, SUB, SIDE), F32)
    for number in range(CHANNELS):
        rate = jnp.where(kind == float(number), scales_ref[CHANNELS + number], rate)
    rate = rate.reshape(SIDE, SIDE)

    pressure = jnp.zeros((SIDE, SIDE), F32)
    for channel in range(MIXED):
        spread = jnp.dot(
            smoothed[channel].astype(BF16), tables[channel][...], preferred_element_type=F32
        )
        total = None
        for block in range(blocks(channel)):
            term = rolled_rows(
                spread[:, block * SIDE : (block + 1) * SIDE], block - reach(channel)
            )
            total = term if total is None else total + term
        pressure = pressure + scaled(total, scales_ref[channel])
    total = jnp.zeros((SIDE, SIDE), F32)
    for step in range(ROWS):
        total = total + rolled_rows(scaled(smoothed[MIXED], last_ref[step]), step)
    pressure = pressure + scaled(total, scales_ref[MIXED])

    shifted = 1.0 + pressure
    decay = jnp.exp(-jnp.abs(shifted))
    removed = rate * (jnp.maximum(shifted, 0.0) + jnp.log1p(decay))
    slope = jnp.where(shifted >= 0, 1.0, decay) / (1.0 + decay)
    adjoint = (-(away - removed) * rate * slope / SIDE).astype(BF16)

    weighted = []
    gain_rows = []
    for channel in range(CHANNELS):
        total = jnp.zeros((SIDE, SIDE), F32)
        if channel < MIXED:
            for block in range(blocks(channel)):
                term = lax.dot_general(
                    adjoint,
                    tables[channel][:, block * SIDE : (block + 1) * SIDE],
                    (((1,), (1,)), ((), ())),
                    preferred_element_type=F32,
                )
                total = total + rolled_rows(term, reach(channel) - block)
        else:
            wide = adjoint.astype(F32)
            for step in range(ROWS):
                total = total + rolled_rows(scaled(wide, last_ref[step]), -step)
        gain_rows.append(jnp.sum(total * smoothed[channel], axis=0, keepdims=True))
        weighted.append(scaled(total, scales_ref[channel]))
    for pair in range(CHANNELS // 2):
        out_ref[:, 16 * pair : 16 * pair + 16, :] = pair_rows(
            weighted[2 * pair], weighted[2 * pair + 1]
        ).astype(BF16)
    high, low = split(removed)
    out_ref[:, 64:, :] = pair_rows(high.astype(F32), low.astype(F32)).astype(BF16)
    gain_ref[...] = jnp.concatenate(gain_rows, axis=0)


def gradient_kernel(
    place_ref, region_ref, back_ref, own_ref, other_ref, gain_ref, height_in, last_ref, *refs
):
    tables, new_ref, sums_ref = refs[:MIXED], refs[MIXED], refs[MIXED + 1]
    height_ref, sem = refs[MIXED + 2 :]
    copy = pltpu.make_async_copy(height_in, height_ref, sem.at[0])
    copy.start()
    weighted = []
    for pair in range(CHANNELS // 2):
        weighted.extend(unpair_rows(back_ref[:, 16 * pair : 16 * pair + 16, :]))
    turned = weighted[MIXED].T
    narrow = [weighted[channel].astype(BF16) for channel in range(MIXED)]
    here = place_ref[0]
    lane = lax.broadcasted_iota(jnp.int32, (1, SIDE), 1)
    line = jnp.zeros((1, SIDE), F32)
    for step in range(COLS):
        block = lax.rem(here + (COLS - HALF + step), COLS) // 2
        values = (own_ref if step % 2 == 0 else other_ref)[block, SIDE:, :]
        product = turned * values.astype(F32)
        product = jnp.sum(product.reshape(ROWS, SUB, SIDE), axis=0)
        terms = product * last_ref[step]
        ahead = step - HALF
        channels = [c for c in range(MIXED) if abs(ahead) <= reach(c)]
        for channel in channels:
            first = (ahead + reach(channel)) * SIDE
            cross = jnp.dot(narrow[channel], values, preferred_element_type=F32)
            taps = tables[channel][:, first : first + SIDE].astype(F32)
            terms = terms + jnp.sum((cross * taps).reshape(ROWS, SUB, SIDE), axis=0)
        total = jnp.sum(jnp.sum(terms, axis=0, keepdims=True), axis=1, keepdims=True)
        line = line + jnp.where(lane == step, total, 0.0)
    gain = jnp.sum(gain_ref[...], axis=1, keepdims=True)
    row = lax.broadcasted_iota(jnp.int32, (SUB, SIDE), 0)
    wide_lane = lax.broadcasted_iota(jnp.int32, (SUB, SIDE), 1)
    gain = jnp.sum(jnp.where(row + COLS == wide_lane, gain, 0.0), axis=0, keepdims=True)
    region = region_ref[0, 0].astype(F32)
    line = line + gain + jnp.where(lane == COLS + SUB, region, 0.0)
    for peer in range(COLS):
        sums_ref[peer] = line
    high, low = unpair_rows(back_ref[:, 64:80, :])
    copy.wait()
    new_ref[...] = height_ref[...] - (high + low).T


def regions_kernel(place_ref, lines_ref, out_ref):
    lines = lines_ref[...].reshape(COLS, SIDE)
    sender = lax.broadcasted_iota(jnp.int32, (COLS, SIDE), 0)
    lane = lax.broadcasted_iota(jnp.int32, (COLS, SIDE), 1)
    sums = jnp.where(lane < COLS, lines, 0.0)
    region = jnp.sum(jnp.where(lane == COLS + SUB, lines, 0.0), axis=1, keepdims=True)
    gain = jnp.sum(jnp.where((lane >= COLS) & (lane < COLS + SUB), lines, 0.0), axis=0, keepdims=True)
    fill = jnp.zeros((1, SIDE), F32)
    for block in range(COLS):
        held = jnp.sum(jnp.where(lane == lax.rem(block + HALF - sender + COLS, COLS), sums, 0.0))
        fill = fill + jnp.where(region[block : block + 1] == lane[:1].astype(F32), held, 0.0)
    both = jnp.concatenate([fill, gain], axis=0)
    for peer in range(ROWS):
        out_ref[peer] = both


def total_kernel(sums_ref, fill_ref, gain_ref):
    total = jnp.sum(sums_ref[...], axis=0)
    fill_ref[...] = total[0]
    gain_ref[...] = total[1, COLS : COLS + CHANNELS]


def shape(*dims, dtype=F32):
    return jax.ShapeDtypeStruct(dims, dtype)


def shards(
    height,
    density,
    target,
    region_of_block,
    class_of_block,
    fill_level,
    rates,
    col_taps,
    row_taps,
    gains,
):
    place = lax.axis_index("col").astype(jnp.int32).reshape(1)
    copies = pl.pallas_call(
        source_kernel,
        out_shape=shape(PEERS, 2 * SIDE, SIDE, dtype=BF16),
        in_specs=[SMEM, SMEM, HBM, HBM, HBM],
        out_specs=VMEM,
        scratch_shapes=[
            pltpu.SMEM((SIDE,), F32),
            pltpu.VMEM((SIDE, SIDE), F32),
            pltpu.VMEM((SIDE, SIDE), F32),
            pltpu.SemaphoreType.DMA((3,)),
        ],
        compiler_params=pltpu.CompilerParams(vmem_limit_bytes=60 * 1024 * 1024),
        name="source",
    )(place, region_of_block, fill_level, height, density)
    groups = [[2 * block + core for block in range(PEERS)] for core in range(2)]
    own = lax.all_to_all(copies, "col", 0, 0, axis_index_groups=groups, tiled=True)
    other = lax.ppermute(own, "col", [(block, block ^ 1) for block in range(COLS)])
    table_shapes = [shape(SIDE, blocks(c) * SIDE, dtype=BF16) for c in range(MIXED)]
    made = pl.pallas_call(
        tables_kernel,
        out_shape=table_shapes
        + [shape(COLS, SUB, SIDE)]
        + table_shapes
        + [shape(ROWS, SUB, SIDE), shape(2 * CHANNELS, SUB, SIDE)],
        in_specs=[HBM] * 4 + [ANY],
        out_specs=[VMEM] * (2 * MIXED + 3),
        scratch_shapes=[
            pltpu.SMEM((CHANNELS, TAPS), F32),
            pltpu.SMEM((CHANNELS, TAPS), F32),
            pltpu.SMEM((CHANNELS,), F32),
            pltpu.SMEM((CHANNELS,), F32),
            pltpu.SemaphoreType.DMA((4,)),
        ],
        compiler_params=PARAMS,
        cost_estimate=pl.CostEstimate(flops=4000000, bytes_accessed=4000000, transcendentals=0),
        name="tables",
    )(col_taps, row_taps, gains, rates, own)
    col_tables, col_last = made[:MIXED], made[MIXED]
    row_tables, row_last = made[MIXED + 1 : 2 * MIXED + 1], made[2 * MIXED + 1]
    scales = made[2 * MIXED + 2]

    smoothed = pl.pallas_call(
        smooth_kernel,
        out_shape=shape(ROWS, 80, SIDE, dtype=BF16),
        in_specs=[SMEM, SMEM, VMEM, VMEM, HBM, HBM] + [VMEM] * (1 + MIXED),
        out_specs=VMEM,
        scratch_shapes=[
            pltpu.VMEM((COLS * SIDE, SIDE), BF16),
            pltpu.VMEM((SIDE, SIDE), F32),
            pltpu.VMEM((SIDE, SIDE), F32),
            pltpu.SemaphoreType.DMA((2,)),
        ],
        compiler_params=PARAMS,
        name="smooth",
    )(place, class_of_block, own, other, height, target, col_last, *col_tables)
    long = lax.all_to_all(smoothed, "row", 0, 0, tiled=True)

    back, gain_part = pl.pallas_call(
        pressure_kernel,
        out_shape=[shape(ROWS, 80, SIDE, dtype=BF16), shape(CHANNELS, SIDE)],
        in_specs=[VMEM] * (3 + MIXED),
        out_specs=[VMEM, VMEM],
        compiler_params=PARAMS,
        name="pressure",
    )(scales, long, row_last, *row_tables)
    tile = lax.all_to_all(back, "row", 0, 0, tiled=True)
    new_height, lines = pl.pallas_call(
        gradient_kernel,
        out_shape=[shape(SIDE, SIDE), shape(COLS, 1, SIDE)],
        in_specs=[SMEM, SMEM] + [VMEM] * 4 + [HBM] + [VMEM] * (1 + MIXED),
        out_specs=[VMEM, VMEM],
        scratch_shapes=[pltpu.VMEM((SIDE, SIDE), F32), pltpu.SemaphoreType.DMA((1,))],
        compiler_params=PARAMS,
        name="gradient",
    )(place, region_of_block, tile, own, other, gain_part, height, col_last, *col_tables)
    by_col = lax.all_to_all(lines, "col", 0, 0, tiled=True)
    sums = pl.pallas_call(
        regions_kernel,
        out_shape=shape(ROWS, 2, SIDE),
        in_specs=[SMEM, VMEM],
        out_specs=VMEM,
        compiler_params=PARAMS,
        name="regions",
    )(place, by_col)
    by_row = lax.all_to_all(sums, "row", 0, 0, tiled=True)
    fill_grad, gain_grad = pl.pallas_call(
        total_kernel,
        out_shape=[shape(SIDE), shape(CHANNELS)],
        in_specs=[VMEM],
        out_specs=[VMEM, VMEM],
        compiler_params=PARAMS,
        name="total",
    )(by_row)
    return new_height, gain_grad, fill_grad


def solution(mesh):
    cells = P("row", "col")
    in_specs = (cells,) * 5 + (P(),) * 5
    out_specs = (cells, P(), P())
    return jax.shard_map(shards, mesh=mesh, in_specs=in_specs, out_specs=out_specs, check_vma=False)
```

```python
import functools

import jax
import jax.numpy as jnp
from jax import lax
from jax.experimental import pallas as pl
from jax.experimental.pallas import tpu as pltpu
from jax.sharding import PartitionSpec as P

CHANNELS = 8
TAPS = 33
HALF = TAPS // 2
SIDE = 128
ROWS = 16
COLS = 32
PEERS = COLS // 2
SUB = SIDE // ROWS
MIXED = CHANNELS - 1
F32 = jnp.float32
BF16 = jnp.bfloat16
VMEM = pl.BlockSpec(memory_space=pltpu.VMEM)
SMEM = pl.BlockSpec(memory_space=pltpu.SMEM)
ANY = pl.BlockSpec(memory_space=pl.ANY)
HBM = pl.BlockSpec(memory_space=pltpu.HBM)
PARAMS = pltpu.CompilerParams(vmem_limit_bytes=24 * 1024 * 1024)


def reach(channel):
    return max(1, 2**channel * HALF // SIDE)


def blocks(channel):
    return 2 * reach(channel) + 1


def split(values):
    high = values.astype(BF16)
    low = (values - high.astype(F32)).astype(BF16)
    return high, low


def pair_rows(first, second):
    return jnp.concatenate(
        [first.reshape(ROWS, SUB, SIDE), second.reshape(ROWS, SUB, SIDE)], axis=1
    )


def unpair_rows(pairs):
    values = pairs.astype(F32)
    return (
        values[:, :SUB, :].reshape(SIDE, SIDE),
        values[:, SUB:, :].reshape(SIDE, SIDE),
    )


def scaled(values, scale):
    return (values.reshape(ROWS, SUB, SIDE) * scale).reshape(SIDE, SIDE)


def fetch(sources, targets, sem):
    copies = [
        pltpu.make_async_copy(source, target, sem.at[number])
        for number, (source, target) in enumerate(zip(sources, targets))
    ]
    for copy in copies:
        copy.start()
    for copy in copies:
        copy.wait()


def scatter_round(values, place):
    near = values.astype(BF16).astype(F32)
    step = (near * (1.0 + 0.7 / 128)).astype(BF16).astype(F32) - near
    row = lax.broadcasted_iota(jnp.int32, values.shape, 0).astype(F32)
    column = lax.broadcasted_iota(jnp.int32, values.shape, 1).astype(F32)
    mixed = row * 0.7548777 + column * 0.5698403 + place.astype(F32) * 0.6180340
    return (values + step * (mixed - jnp.floor(mixed) - 0.5)).astype(BF16)


def source_kernel(place_ref, region_ref, fill_in, height_in, density_in, out_ref, *scratch):
    fill_ref, height_ref, density_ref, sem = scratch
    fetch((fill_in, height_in, density_in), (fill_ref, height_ref, density_ref), sem)
    fill = fill_ref[region_ref[0, 0]]
    height = height_ref[...]
    source = (density_ref[...] + fill) * height
    turned = source.T.astype(BF16)
    rounded = scatter_round(height, place_ref[0])
    for peer in range(PEERS):
        out_ref[peer, :SIDE, :] = turned
        out_ref[peer, SIDE:, :] = rounded


def toeplitz(taps_ref, channel, direction, merged):
    width = (blocks(channel) + 1) * SIDE
    lane = lax.broadcasted_iota(jnp.int32, (1, SIDE), 1)
    parts = [jnp.zeros((1, SIDE), F32) for _ in range(width // SIDE)]
    for position in range(TAPS):
        value = taps_ref[channel, position]
        if merged and position == 0:
            continue
        if merged and position == TAPS - 1:
            value = value + taps_ref[channel, 0]
        place = reach(channel) * SIDE + direction * (position - HALF) * 2**channel
        part, inside = divmod(place, SIDE)
        parts[part] = jnp.where(lane == inside, value, parts[part])
    base = jnp.concatenate(parts, axis=1).astype(BF16).astype(F32)
    spread = jnp.broadcast_to(base, (SIDE, width))
    rolled = pltpu.roll(spread, 0, 1, stride=1, stride_axis=0)
    return rolled[:, : blocks(channel) * SIDE].astype(BF16)


def fill_tables(taps_ref, outs, last_ref, direction, merged):
    for channel in range(MIXED):
        outs[channel][...] = toeplitz(taps_ref, channel, direction, merged and channel == 6)
    steps = last_ref.shape[0]
    for step in range(steps):
        places = [t for t in range(TAPS) if (direction * (t - HALF) + HALF - step) % steps == 0]
        value = taps_ref[MIXED, places[0]]
        for place in places[1:]:
            value = value + taps_ref[MIXED, place]
        last_ref[step] = jnp.full((SUB, SIDE), value, F32).astype(BF16).astype(F32)


def tables_kernel(col_in, row_in, gains_in, rates_in, after_ref, *refs):
    scales_ref, col_ref, row_ref, gains_ref, rates_ref, sem = refs[2 * MIXED + 2 :]
    fetch(
        (col_in, row_in, gains_in, rates_in), (col_ref, row_ref, gains_ref, rates_ref), sem
    )
    for number in range(CHANNELS):
        scales_ref[number] = jnp.full((SUB, SIDE), gains_ref[number], F32)
        scales_ref[CHANNELS + number] = jnp.full((SUB, SIDE), rates_ref[number], F32)
    fill_tables(col_ref, refs[:MIXED], refs[MIXED], -1, False)
    fill_tables(row_ref, refs[MIXED + 1 : 2 * MIXED + 1], refs[2 * MIXED + 1], 1, True)


def smooth_kernel(place_ref, class_ref, own_ref, other_ref, height_in, target_in, last_ref, *refs):
    tables, out_ref = refs[:MIXED], refs[MIXED]
    window_ref, height_ref, target_ref, sem = refs[MIXED + 1 :]
    copies = [
        pltpu.make_async_copy(height_in, height_ref, sem.at[0]),
        pltpu.make_async_copy(target_in, target_ref, sem.at[1]),
    ]
    for copy in copies:
        copy.start()
    here = place_ref[0]
    last = jnp.zeros((SIDE, SIDE), F32)
    for step in range(COLS):
        block = lax.rem(here + (COLS - HALF + step), COLS) // 2
        chunk_ref = own_ref if step % 2 == 0 else other_ref
        values = chunk_ref[block, :SIDE, :]
        window_ref[step * SIDE : (step + 1) * SIDE, :] = values
        last = last + scaled(values.astype(F32), last_ref[step])
    smoothed = []
    for channel in range(MIXED):
        first = (HALF - reach(channel)) * SIDE
        smoothed.append(
            jnp.dot(
                tables[channel][...],
                window_ref[first : first + blocks(channel) * SIDE, :],
                preferred_element_type=F32,
            )
        )
    smoothed.append(last)
    for pair in range(CHANNELS // 2):
        out_ref[:, 16 * pair : 16 * pair + 16, :] = pair_rows(
            smoothed[2 * pair], smoothed[2 * pair + 1]
        ).astype(BF16)
    for copy in copies:
        copy.wait()
    away = (height_ref[...] - target_ref[...]).T
    high, low = split(away)
    row = lax.broadcasted_iota(jnp.int32, (SIDE, SIDE), 0)
    lane = lax.broadcasted_iota(jnp.int32, (SIDE, SIDE), 1)
    first = (row % SUB == 0) & (lane == 0)
    low = jnp.where(first, class_ref[0, 0].astype(F32), low.astype(F32))
    out_ref[:, 64:, :] = pair_rows(high.astype(F32), low).astype(BF16)


def rolled_rows(values, block_shift):
    shift = block_shift * SUB % SIDE
    if shift == 0:
        return values
    return jnp.concatenate([values[SIDE - shift :], values[: SIDE - shift]], axis=0)


def pressure_kernel(scales_ref, long_ref, last_ref, *refs):
    tables, out_ref, gain_ref = refs[:MIXED], refs[MIXED], refs[MIXED + 1]
    smoothed = []
    for pair in range(CHANNELS // 2):
        smoothed.extend(unpair_rows(long_ref[:, 16 * pair : 16 * pair + 16, :]))
    high, low = unpair_rows(long_ref[:, 64:, :])
    low = low.reshape(ROWS, SUB, SIDE)
    row = lax.broadcasted_iota(jnp.int32, (ROWS, SUB, SIDE), 1)
    lane = lax.broadcasted_iota(jnp.int32, (ROWS, SUB, SIDE), 2)
    first = (row == 0) & (lane == 0)
    kind = jnp.max(jnp.where(first, low, 0.0), axis=(1, 2), keepdims=True)
    away = high + jnp.where(first, 0.0, low).reshape(SIDE, SIDE)
    rate = jnp.zeros((ROWS, SUB, SIDE), F32)
    for number in range(CHANNELS):
        rate = jnp.where(kind == float(number), scales_ref[CHANNELS + number], rate)
    rate = rate.reshape(SIDE, SIDE)

    pressure = jnp.zeros((SIDE, SIDE), F32)
    for channel in range(MIXED):
        spread = jnp.dot(
            smoothed[channel].astype(BF16), tables[channel][...], preferred_element_type=F32
        )
        total = None
        for block in range(blocks(channel)):
            term = rolled_rows(
                spread[:, block * SIDE : (block + 1) * SIDE], block - reach(channel)
            )
            total = term if total is None else total + term
        pressure = pressure + scaled(total, scales_ref[channel])
    total = jnp.zeros((SIDE, SIDE), F32)
    for step in range(ROWS):
        total = total + rolled_rows(scaled(smoothed[MIXED], last_ref[step]), step)
    pressure = pressure + scaled(total, scales_ref[MIXED])

    shifted = 1.0 + pressure
    decay = jnp.exp(-jnp.abs(shifted))
    removed = rate * (jnp.maximum(shifted, 0.0) + jnp.log1p(decay))
    slope = jnp.where(shifted >= 0, 1.0, decay) / (1.0 + decay)
    adjoint = (-(away - removed) * rate * slope / SIDE).astype(BF16)

    weighted = []
    gain_rows = []
    for channel in range(CHANNELS):
        total = jnp.zeros((SIDE, SIDE), F32)
        if channel < MIXED:
            for block in range(blocks(channel)):
                term = lax.dot_general(
                    adjoint,
                    tables[channel][:, block * SIDE : (block + 1) * SIDE],
                    (((1,), (1,)), ((), ())),
                    preferred_element_type=F32,
                )
                total = total + rolled_rows(term, reach(channel) - block)
        else:
            wide = adjoint.astype(F32)
            for step in range(ROWS):
                total = total + rolled_rows(scaled(wide, last_ref[step]), -step)
        gain_rows.append(jnp.sum(total * smoothed[channel], axis=0, keepdims=True))
        weighted.append(scaled(total, scales_ref[channel]))
    for pair in range(CHANNELS // 2):
        out_ref[:, 16 * pair : 16 * pair + 16, :] = pair_rows(
            weighted[2 * pair], weighted[2 * pair + 1]
        ).astype(BF16)
    high, low = split(removed)
    out_ref[:, 64:, :] = pair_rows(high.astype(F32), low.astype(F32)).astype(BF16)
    gain_ref[...] = jnp.concatenate(gain_rows, axis=0)


def gradient_kernel(
    place_ref, region_ref, back_ref, own_ref, other_ref, gain_ref, last_ref, *refs
):
    tables, sums_ref = refs[:MIXED], refs[MIXED]
    weighted = []
    for pair in range(CHANNELS // 2):
        weighted.extend(unpair_rows(back_ref[:, 16 * pair : 16 * pair + 16, :]))
    turned = weighted[MIXED].T
    narrow = [weighted[channel].astype(BF16) for channel in range(MIXED)]
    here = place_ref[0]
    parts = []
    for step in range(COLS):
        block = lax.rem(here + (COLS - HALF + step), COLS) // 2
        values = (own_ref if step % 2 == 0 else other_ref)[block, SIDE:, :]
        product = turned * values.astype(F32)
        product = jnp.sum(product.reshape(ROWS, SUB, SIDE), axis=0)
        terms = product * last_ref[step]
        ahead = step - HALF
        channels = [c for c in range(MIXED) if abs(ahead) <= reach(c)]
        for channel in channels:
            first = (ahead + reach(channel)) * SIDE
            cross = jnp.dot(narrow[channel], values, preferred_element_type=F32)
            taps = tables[channel][:, first : first + SIDE].astype(F32)
            terms = terms + jnp.sum((cross * taps).reshape(ROWS, SUB, SIDE), axis=0)
        parts.append(terms)
    total = jnp.sum(jnp.concatenate(parts, axis=0), axis=1, keepdims=True)
    row = lax.broadcasted_iota(jnp.int32, (COLS * SUB, SIDE), 0)
    lane = lax.broadcasted_iota(jnp.int32, (COLS * SUB, SIDE), 1)
    block = lax.rem(here + HALF + row // SUB, COLS)
    line = jnp.sum(jnp.where(lane == block, total, 0.0), axis=0, keepdims=True)
    gain = jnp.sum(gain_ref[...], axis=1, keepdims=True)
    gain = jnp.where(lane[:SUB] == COLS + row[:SUB], gain, 0.0)
    region = region_ref[0, 0].astype(F32)
    line = line + jnp.sum(gain, axis=0, keepdims=True)
    line = line + jnp.where(lane[:1] == 2 * COLS, region, 0.0)
    for peer in range(COLS):
        sums_ref[peer] = line


def band_kernel(lines_ref, out_ref):
    lines = lines_ref[...].reshape(COLS, SIDE)
    row = lax.broadcasted_iota(jnp.int32, (COLS, SIDE), 0)
    lane = lax.broadcasted_iota(jnp.int32, (COLS, SIDE), 1)
    band = jnp.sum(lines, axis=0, keepdims=True)
    held = jnp.sum(jnp.where(lane == row, band, 0.0), axis=1, keepdims=True)
    region = jnp.sum(jnp.where(lane == 2 * COLS, lines, 0.0), axis=1, keepdims=True)
    fill = jnp.where(region == lane.astype(F32), held, 0.0)
    both = jnp.concatenate([jnp.sum(fill, axis=0, keepdims=True), band], axis=0)
    for peer in range(ROWS):
        out_ref[peer] = both


def total_kernel(bands_ref, back_ref, height_ref, new_ref, fill_ref, gain_ref):
    total = jnp.sum(bands_ref[...], axis=0)
    fill_ref[...] = total[0]
    gain_ref[...] = total[1, COLS : COLS + CHANNELS]
    high, low = unpair_rows(back_ref[:, 64:80, :])
    new_ref[...] = height_ref[...] - (high + low).T


def shape(*dims, dtype=F32):
    return jax.ShapeDtypeStruct(dims, dtype)


def shards(
    height,
    density,
    target,
    region_of_block,
    class_of_block,
    fill_level,
    rates,
    col_taps,
    row_taps,
    gains,
):
    place = lax.axis_index("col").astype(jnp.int32).reshape(1)
    copies = pl.pallas_call(
        source_kernel,
        out_shape=shape(PEERS, 2 * SIDE, SIDE, dtype=BF16),
        in_specs=[SMEM, SMEM, HBM, HBM, HBM],
        out_specs=VMEM,
        scratch_shapes=[
            pltpu.SMEM((SIDE,), F32),
            pltpu.VMEM((SIDE, SIDE), F32),
            pltpu.VMEM((SIDE, SIDE), F32),
            pltpu.SemaphoreType.DMA((3,)),
        ],
        compiler_params=pltpu.CompilerParams(vmem_limit_bytes=60 * 1024 * 1024),
        name="source",
    )(place, region_of_block, fill_level, height, density)
    groups = [[2 * block + core for block in range(PEERS)] for core in range(2)]
    own = lax.all_to_all(copies, "col", 0, 0, axis_index_groups=groups, tiled=True)
    other = lax.ppermute(own, "col", [(block, block ^ 1) for block in range(COLS)])
    table_shapes = [shape(SIDE, blocks(c) * SIDE, dtype=BF16) for c in range(MIXED)]
    made = pl.pallas_call(
        tables_kernel,
        out_shape=table_shapes
        + [shape(COLS, SUB, SIDE)]
        + table_shapes
        + [shape(ROWS, SUB, SIDE), shape(2 * CHANNELS, SUB, SIDE)],
        in_specs=[HBM] * 4 + [ANY],
        out_specs=[VMEM] * (2 * MIXED + 3),
        scratch_shapes=[
            pltpu.SMEM((CHANNELS, TAPS), F32),
            pltpu.SMEM((CHANNELS, TAPS), F32),
            pltpu.SMEM((CHANNELS,), F32),
            pltpu.SMEM((CHANNELS,), F32),
            pltpu.SemaphoreType.DMA((4,)),
        ],
        compiler_params=PARAMS,
        cost_estimate=pl.CostEstimate(flops=4000000, bytes_accessed=4000000, transcendentals=0),
        name="tables",
    )(col_taps, row_taps, gains, rates, own)
    col_tables, col_last = made[:MIXED], made[MIXED]
    row_tables, row_last = made[MIXED + 1 : 2 * MIXED + 1], made[2 * MIXED + 1]
    scales = made[2 * MIXED + 2]

    smoothed = pl.pallas_call(
        smooth_kernel,
        out_shape=shape(ROWS, 80, SIDE, dtype=BF16),
        in_specs=[SMEM, SMEM, VMEM, VMEM, HBM, HBM] + [VMEM] * (1 + MIXED),
        out_specs=VMEM,
        scratch_shapes=[
            pltpu.VMEM((COLS * SIDE, SIDE), BF16),
            pltpu.VMEM((SIDE, SIDE), F32),
            pltpu.VMEM((SIDE, SIDE), F32),
            pltpu.SemaphoreType.DMA((2,)),
        ],
        compiler_params=PARAMS,
        name="smooth",
    )(place, class_of_block, own, other, height, target, col_last, *col_tables)
    long = lax.all_to_all(smoothed, "row", 0, 0, tiled=True)

    back, gain_part = pl.pallas_call(
        pressure_kernel,
        out_shape=[shape(ROWS, 80, SIDE, dtype=BF16), shape(CHANNELS, SIDE)],
        in_specs=[VMEM] * (3 + MIXED),
        out_specs=[VMEM, VMEM],
        compiler_params=PARAMS,
        name="pressure",
    )(scales, long, row_last, *row_tables)
    tile = lax.all_to_all(back, "row", 0, 0, tiled=True)
    lines = pl.pallas_call(
        gradient_kernel,
        out_shape=shape(COLS, 1, SIDE),
        in_specs=[SMEM, SMEM] + [VMEM] * (5 + MIXED),
        out_specs=VMEM,
        compiler_params=PARAMS,
        name="gradient",
    )(place, region_of_block, tile, own, other, gain_part, col_last, *col_tables)
    by_col = lax.all_to_all(lines, "col", 0, 0, tiled=True)
    bands = pl.pallas_call(
        band_kernel,
        out_shape=shape(ROWS, 2, SIDE),
        in_specs=[VMEM],
        out_specs=VMEM,
        compiler_params=PARAMS,
        name="band",
    )(by_col)
    by_row = lax.all_to_all(bands, "row", 0, 0, tiled=True)
    new_height, fill_grad, gain_grad = pl.pallas_call(
        total_kernel,
        out_shape=[shape(SIDE, SIDE), shape(SIDE), shape(CHANNELS)],
        in_specs=[VMEM] * 3,
        out_specs=[VMEM] * 3,
        compiler_params=PARAMS,
        name="total",
    )(by_row, tile, height)
    return new_height, gain_grad, fill_grad


def solution(mesh):
    cells = P("row", "col")
    in_specs = (cells,) * 5 + (P(),) * 5
    out_specs = (cells, P(), P())
    return jax.shard_map(shards, mesh=mesh, in_specs=in_specs, out_specs=out_specs, check_vma=False)
```

```python
import functools

import jax
import jax.numpy as jnp
from jax import lax
from jax.experimental import pallas as pl
from jax.experimental.pallas import tpu as pltpu
from jax.sharding import PartitionSpec as P

CHANNELS = 8
TAPS = 33
HALF = TAPS // 2
SIDE = 128
ROWS = 16
COLS = 32
PEERS = COLS // 2
SUB = SIDE // ROWS
MIXED = CHANNELS - 1
F32 = jnp.float32
BAND_ORDER = [2 * step + half for half in range(2) for step in range(ROWS // 2)]
BF16 = jnp.bfloat16
VMEM = pl.BlockSpec(memory_space=pltpu.VMEM)
SMEM = pl.BlockSpec(memory_space=pltpu.SMEM)
ANY = pl.BlockSpec(memory_space=pl.ANY)
HBM = pl.BlockSpec(memory_space=pltpu.HBM)
PARAMS = pltpu.CompilerParams(vmem_limit_bytes=24 * 1024 * 1024)


def reach(channel):
    return max(1, 2**channel * HALF // SIDE)


def blocks(channel):
    return 2 * reach(channel) + 1


def split(values):
    high = values.astype(BF16)
    low = (values - high.astype(F32)).astype(BF16)
    return high, low


def pair_rows(first, second):
    return jnp.concatenate(
        [first.reshape(ROWS, SUB, SIDE), second.reshape(ROWS, SUB, SIDE)], axis=1
    )


def unpair_rows(pairs):
    values = pairs.astype(F32)
    return (
        values[:, :SUB, :].reshape(SIDE, SIDE),
        values[:, SUB:, :].reshape(SIDE, SIDE),
    )


def along_rows(values):
    return jnp.concatenate(
        [values[SUB * p : SUB * p + SUB] for p in (b % 2 * (ROWS // 2) + b // 2 for b in range(ROWS))],
        axis=0,
    )


def along_peers(values):
    return jnp.concatenate(
        [values[SUB * b : SUB * b + SUB] for b in BAND_ORDER], axis=0
    )


def scaled(values, scale):
    return (values.reshape(ROWS, SUB, SIDE) * scale).reshape(SIDE, SIDE)


def fetch(sources, targets, sem):
    copies = [
        pltpu.make_async_copy(source, target, sem.at[number])
        for number, (source, target) in enumerate(zip(sources, targets))
    ]
    for copy in copies:
        copy.start()
    for copy in copies:
        copy.wait()


def scatter_round(values, place):
    near = values.astype(BF16).astype(F32)
    step = (near * (1.0 + 0.7 / 128)).astype(BF16).astype(F32) - near
    row = lax.broadcasted_iota(jnp.int32, values.shape, 0).astype(F32)
    column = lax.broadcasted_iota(jnp.int32, values.shape, 1).astype(F32)
    mixed = row * 0.7548777 + column * 0.5698403 + place.astype(F32) * 0.6180340
    return (values + step * (mixed - jnp.floor(mixed) - 0.5)).astype(BF16)


def source_kernel(place_ref, region_ref, fill_in, height_in, density_in, out_ref, *scratch):
    fill_ref, height_ref, density_ref, sem = scratch
    fetch((fill_in, height_in, density_in), (fill_ref, height_ref, density_ref), sem)
    fill = fill_ref[region_ref[0, 0]]
    height = height_ref[...]
    source = (density_ref[...] + fill) * height
    turned = source.T.astype(BF16)
    rounded = scatter_round(height, place_ref[0])
    for peer in range(PEERS):
        out_ref[peer, :SIDE, :] = turned
        out_ref[peer, SIDE:, :] = rounded


def toeplitz(taps_ref, channel, direction, merged):
    width = (blocks(channel) + 1) * SIDE
    lane = lax.broadcasted_iota(jnp.int32, (1, SIDE), 1)
    parts = [jnp.zeros((1, SIDE), F32) for _ in range(width // SIDE)]
    for position in range(TAPS):
        value = taps_ref[channel, position]
        if merged and position == 0:
            continue
        if merged and position == TAPS - 1:
            value = value + taps_ref[channel, 0]
        place = reach(channel) * SIDE + direction * (position - HALF) * 2**channel
        part, inside = divmod(place, SIDE)
        parts[part] = jnp.where(lane == inside, value, parts[part])
    base = jnp.concatenate(parts, axis=1).astype(BF16).astype(F32)
    spread = jnp.broadcast_to(base, (SIDE, width))
    rolled = pltpu.roll(spread, 0, 1, stride=1, stride_axis=0)
    return rolled[:, : blocks(channel) * SIDE].astype(BF16)


def fill_tables(taps_ref, outs, last_ref, direction, merged):
    for channel in range(MIXED):
        outs[channel][...] = toeplitz(taps_ref, channel, direction, merged and channel == 6)
    steps = last_ref.shape[0]
    for step in range(steps):
        places = [t for t in range(TAPS) if (direction * (t - HALF) + HALF - step) % steps == 0]
        value = taps_ref[MIXED, places[0]]
        for place in places[1:]:
            value = value + taps_ref[MIXED, place]
        last_ref[step] = jnp.full((SUB, SIDE), value, F32).astype(BF16).astype(F32)


def tables_kernel(col_in, row_in, gains_in, rates_in, after_ref, *refs):
    scales_ref, col_ref, row_ref, gains_ref, rates_ref, sem = refs[2 * MIXED + 2 :]
    fetch(
        (col_in, row_in, gains_in, rates_in), (col_ref, row_ref, gains_ref, rates_ref), sem
    )
    for number in range(CHANNELS):
        scales_ref[number] = jnp.full((SUB, SIDE), gains_ref[number], F32)
        scales_ref[CHANNELS + number] = jnp.full((SUB, SIDE), rates_ref[number], F32)
    fill_tables(col_ref, refs[:MIXED], refs[MIXED], -1, False)
    fill_tables(row_ref, refs[MIXED + 1 : 2 * MIXED + 1], refs[2 * MIXED + 1], 1, True)


def smooth_kernel(place_ref, class_ref, own_ref, other_ref, height_in, target_in, last_ref, *refs):
    tables, out_ref = refs[:MIXED], refs[MIXED]
    window_ref, height_ref, target_ref, sem = refs[MIXED + 1 :]
    copies = [
        pltpu.make_async_copy(height_in, height_ref, sem.at[0]),
        pltpu.make_async_copy(target_in, target_ref, sem.at[1]),
    ]
    for copy in copies:
        copy.start()
    here = place_ref[0]
    last = jnp.zeros((SIDE, SIDE), F32)
    for step in range(COLS):
        block = lax.rem(here + (COLS - HALF + step), COLS) // 2
        chunk_ref = own_ref if step % 2 == 0 else other_ref
        values = chunk_ref[block, :SIDE, :]
        window_ref[step * SIDE : (step + 1) * SIDE, :] = values
        last = last + scaled(values.astype(F32), last_ref[step])
    smoothed = []
    for channel in range(MIXED):
        first = (HALF - reach(channel)) * SIDE
        smoothed.append(
            jnp.dot(
                tables[channel][...],
                window_ref[first : first + blocks(channel) * SIDE, :],
                preferred_element_type=F32,
            )
        )
    smoothed.append(last)
    for pair in range(CHANNELS // 2):
        out_ref[:, 16 * pair : 16 * pair + 16, :] = pair_rows(
            smoothed[2 * pair], smoothed[2 * pair + 1]
        ).astype(BF16)
    for copy in copies:
        copy.wait()
    away = (height_ref[...] - target_ref[...]).T
    high, low = split(away)
    row = lax.broadcasted_iota(jnp.int32, (SIDE, SIDE), 0)
    lane = lax.broadcasted_iota(jnp.int32, (SIDE, SIDE), 1)
    first = (row % SUB == 0) & (lane == 0)
    low = jnp.where(first, class_ref[0, 0].astype(F32), low.astype(F32))
    out_ref[:, 64:, :] = pair_rows(high.astype(F32), low).astype(BF16)


def rolled_rows(values, block_shift):
    shift = block_shift * SUB % SIDE
    if shift == 0:
        return values
    return jnp.concatenate([values[SIDE - shift :], values[: SIDE - shift]], axis=0)


def pressure_kernel(scales_ref, long_ref, last_ref, *refs):
    tables, out_ref, gain_ref = refs[:MIXED], refs[MIXED], refs[MIXED + 1]
    smoothed = []
    for pair in range(CHANNELS // 2):
        for values in unpair_rows(long_ref[:, 16 * pair : 16 * pair + 16, :]):
            smoothed.append(along_rows(values))
    high, low = map(along_rows, unpair_rows(long_ref[:, 64:, :]))
    low = low.reshape(ROWS, SUB, SIDE)
    row = lax.broadcasted_iota(jnp.int32, (ROWS, SUB, SIDE), 1)
    lane = lax.broadcasted_iota(jnp.int32, (ROWS, SUB, SIDE), 2)
    first = (row == 0) & (lane == 0)
    kind = jnp.max(jnp.where(first, low, 0.0), axis=(1, 2), keepdims=True)
    away = high + jnp.where(first, 0.0, low).reshape(SIDE, SIDE)
    rate = jnp.zeros((ROWS, SUB, SIDE), F32)
    for number in range(CHANNELS):
        rate = jnp.where(kind == float(number), scales_ref[CHANNELS + number], rate)
    rate = rate.reshape(SIDE, SIDE)

    pressure = jnp.zeros((SIDE, SIDE), F32)
    for channel in range(MIXED):
        spread = jnp.dot(
            smoothed[channel].astype(BF16), tables[channel][...], preferred_element_type=F32
        )
        total = None
        for block in range(blocks(channel)):
            term = rolled_rows(
                spread[:, block * SIDE : (block + 1) * SIDE], block - reach(channel)
            )
            total = term if total is None else total + term
        pressure = pressure + scaled(total, scales_ref[channel])
    total = jnp.zeros((SIDE, SIDE), F32)
    for step in range(ROWS):
        total = total + rolled_rows(scaled(smoothed[MIXED], last_ref[step]), step)
    pressure = pressure + scaled(total, scales_ref[MIXED])

    shifted = 1.0 + pressure
    decay = jnp.exp(-jnp.abs(shifted))
    removed = rate * (jnp.maximum(shifted, 0.0) + jnp.log1p(decay))
    slope = jnp.where(shifted >= 0, 1.0, decay) / (1.0 + decay)
    adjoint = (-(away - removed) * rate * slope / SIDE).astype(BF16)

    weighted = []
    gain_rows = []
    for channel in range(CHANNELS):
        total = jnp.zeros((SIDE, SIDE), F32)
        if channel < MIXED:
            for block in range(blocks(channel)):
                term = lax.dot_general(
                    adjoint,
                    tables[channel][:, block * SIDE : (block + 1) * SIDE],
                    (((1,), (1,)), ((), ())),
                    preferred_element_type=F32,
                )
                total = total + rolled_rows(term, reach(channel) - block)
        else:
            wide = adjoint.astype(F32)
            for step in range(ROWS):
                total = total + rolled_rows(scaled(wide, last_ref[step]), -step)
        gain_rows.append(jnp.sum(total * smoothed[channel], axis=0, keepdims=True))
        weighted.append(scaled(total, scales_ref[channel]))
    for pair in range(CHANNELS // 2):
        out_ref[:, 16 * pair : 16 * pair + 16, :] = pair_rows(
            along_peers(weighted[2 * pair]), along_peers(weighted[2 * pair + 1])
        ).astype(BF16)
    high, low = split(along_peers(removed))
    out_ref[:, 64:, :] = pair_rows(high.astype(F32), low.astype(F32)).astype(BF16)
    gain_ref[...] = jnp.concatenate(gain_rows, axis=0)


def gradient_kernel(
    place_ref, region_ref, back_ref, own_ref, other_ref, gain_ref, last_ref, *refs
):
    tables, sums_ref = refs[:MIXED], refs[MIXED]
    weighted = []
    for pair in range(CHANNELS // 2):
        weighted.extend(unpair_rows(back_ref[:, 16 * pair : 16 * pair + 16, :]))
    turned = weighted[MIXED].T
    narrow = [weighted[channel].astype(BF16) for channel in range(MIXED)]
    here = place_ref[0]
    parts = []
    for step in range(COLS):
        block = lax.rem(here + (COLS - HALF + step), COLS) // 2
        values = (own_ref if step % 2 == 0 else other_ref)[block, SIDE:, :]
        product = turned * values.astype(F32)
        product = jnp.sum(product.reshape(ROWS, SUB, SIDE), axis=0)
        terms = product * last_ref[step]
        ahead = step - HALF
        channels = [c for c in range(MIXED) if abs(ahead) <= reach(c)]
        for channel in channels:
            first = (ahead + reach(channel)) * SIDE
            cross = jnp.dot(narrow[channel], values, preferred_element_type=F32)
            taps = tables[channel][:, first : first + SIDE].astype(F32)
            terms = terms + jnp.sum((cross * taps).reshape(ROWS, SUB, SIDE), axis=0)
        parts.append(terms)
    total = jnp.sum(jnp.concatenate(parts, axis=0), axis=1, keepdims=True)
    row = lax.broadcasted_iota(jnp.int32, (COLS * SUB, SIDE), 0)
    lane = lax.broadcasted_iota(jnp.int32, (COLS * SUB, SIDE), 1)
    block = lax.rem(here + HALF + row // SUB, COLS)
    line = jnp.sum(jnp.where(lane == block, total, 0.0), axis=0, keepdims=True)
    gain = jnp.sum(gain_ref[...], axis=1, keepdims=True)
    gain = jnp.where(lane[:SUB] == COLS + row[:SUB], gain, 0.0)
    region = region_ref[0, 0].astype(F32)
    line = line + jnp.sum(gain, axis=0, keepdims=True)
    line = line + jnp.where(lane[:1] == 2 * COLS, region, 0.0)
    for peer in range(COLS):
        sums_ref[peer] = line


def band_kernel(lines_ref, out_ref):
    lines = lines_ref[...].reshape(COLS, SIDE)
    row = lax.broadcasted_iota(jnp.int32, (COLS, SIDE), 0)
    lane = lax.broadcasted_iota(jnp.int32, (COLS, SIDE), 1)
    band = jnp.sum(lines, axis=0, keepdims=True)
    held = jnp.sum(jnp.where(lane == row, band, 0.0), axis=1, keepdims=True)
    region = jnp.sum(jnp.where(lane == 2 * COLS, lines, 0.0), axis=1, keepdims=True)
    fill = jnp.where(region == lane.astype(F32), held, 0.0)
    both = jnp.concatenate([jnp.sum(fill, axis=0, keepdims=True), band], axis=0)
    for peer in range(ROWS):
        out_ref[peer] = both


def total_kernel(bands_ref, back_ref, height_ref, new_ref, fill_ref, gain_ref):
    total = jnp.sum(bands_ref[...], axis=0)
    fill_ref[...] = total[0]
    gain_ref[...] = total[1, COLS : COLS + CHANNELS]
    high, low = unpair_rows(back_ref[:, 64:80, :])
    new_ref[...] = height_ref[...] - (high + low).T


def shape(*dims, dtype=F32):
    return jax.ShapeDtypeStruct(dims, dtype)


def shards(
    height,
    density,
    target,
    region_of_block,
    class_of_block,
    fill_level,
    rates,
    col_taps,
    row_taps,
    gains,
):
    place = lax.axis_index("col").astype(jnp.int32).reshape(1)
    copies = pl.pallas_call(
        source_kernel,
        out_shape=shape(PEERS, 2 * SIDE, SIDE, dtype=BF16),
        in_specs=[SMEM, SMEM, HBM, HBM, HBM],
        out_specs=VMEM,
        scratch_shapes=[
            pltpu.SMEM((SIDE,), F32),
            pltpu.VMEM((SIDE, SIDE), F32),
            pltpu.VMEM((SIDE, SIDE), F32),
            pltpu.SemaphoreType.DMA((3,)),
        ],
        compiler_params=pltpu.CompilerParams(vmem_limit_bytes=60 * 1024 * 1024),
        name="source",
    )(place, region_of_block, fill_level, height, density)
    groups = [[2 * block + core for block in range(PEERS)] for core in range(2)]
    own = lax.all_to_all(copies, "col", 0, 0, axis_index_groups=groups, tiled=True)
    other = lax.ppermute(own, "col", [(block, block ^ 1) for block in range(COLS)])
    table_shapes = [shape(SIDE, blocks(c) * SIDE, dtype=BF16) for c in range(MIXED)]
    made = pl.pallas_call(
        tables_kernel,
        out_shape=table_shapes
        + [shape(COLS, SUB, SIDE)]
        + table_shapes
        + [shape(ROWS, SUB, SIDE), shape(2 * CHANNELS, SUB, SIDE)],
        in_specs=[HBM] * 4 + [ANY],
        out_specs=[VMEM] * (2 * MIXED + 3),
        scratch_shapes=[
            pltpu.SMEM((CHANNELS, TAPS), F32),
            pltpu.SMEM((CHANNELS, TAPS), F32),
            pltpu.SMEM((CHANNELS,), F32),
            pltpu.SMEM((CHANNELS,), F32),
            pltpu.SemaphoreType.DMA((4,)),
        ],
        compiler_params=PARAMS,
        cost_estimate=pl.CostEstimate(flops=4000000, bytes_accessed=4000000, transcendentals=0),
        name="tables",
    )(col_taps, row_taps, gains, rates, own)
    col_tables, col_last = made[:MIXED], made[MIXED]
    row_tables, row_last = made[MIXED + 1 : 2 * MIXED + 1], made[2 * MIXED + 1]
    scales = made[2 * MIXED + 2]

    smoothed = pl.pallas_call(
        smooth_kernel,
        out_shape=shape(ROWS, 80, SIDE, dtype=BF16),
        in_specs=[SMEM, SMEM, VMEM, VMEM, HBM, HBM] + [VMEM] * (1 + MIXED),
        out_specs=VMEM,
        scratch_shapes=[
            pltpu.VMEM((COLS * SIDE, SIDE), BF16),
            pltpu.VMEM((SIDE, SIDE), F32),
            pltpu.VMEM((SIDE, SIDE), F32),
            pltpu.SemaphoreType.DMA((2,)),
        ],
        compiler_params=PARAMS,
        name="smooth",
    )(place, class_of_block, own, other, height, target, col_last, *col_tables)
    long = lax.all_to_all(smoothed, "row", 0, 0, axis_index_groups=[BAND_ORDER], tiled=True)

    back, gain_part = pl.pallas_call(
        pressure_kernel,
        out_shape=[shape(ROWS, 80, SIDE, dtype=BF16), shape(CHANNELS, SIDE)],
        in_specs=[VMEM] * (3 + MIXED),
        out_specs=[VMEM, VMEM],
        compiler_params=PARAMS,
        name="pressure",
    )(scales, long, row_last, *row_tables)
    tile = lax.all_to_all(back, "row", 0, 0, axis_index_groups=[BAND_ORDER], tiled=True)
    lines = pl.pallas_call(
        gradient_kernel,
        out_shape=shape(COLS, 1, SIDE),
        in_specs=[SMEM, SMEM] + [VMEM] * (5 + MIXED),
        out_specs=VMEM,
        compiler_params=PARAMS,
        name="gradient",
    )(place, region_of_block, tile, own, other, gain_part, col_last, *col_tables)
    by_col = lax.all_to_all(lines, "col", 0, 0, tiled=True)
    bands = pl.pallas_call(
        band_kernel,
        out_shape=shape(ROWS, 2, SIDE),
        in_specs=[VMEM],
        out_specs=VMEM,
        compiler_params=PARAMS,
        name="band",
    )(by_col)
    by_row = lax.all_to_all(bands, "row", 0, 0, axis_index_groups=[BAND_ORDER], tiled=True)
    new_height, fill_grad, gain_grad = pl.pallas_call(
        total_kernel,
        out_shape=[shape(SIDE, SIDE), shape(SIDE), shape(CHANNELS)],
        in_specs=[VMEM] * 3,
        out_specs=[VMEM] * 3,
        compiler_params=PARAMS,
        name="total",
    )(by_row, tile, height)
    return new_height, gain_grad, fill_grad


def solution(mesh):
    cells = P("row", "col")
    in_specs = (cells,) * 5 + (P(),) * 5
    out_specs = (cells, P(), P())
    return jax.shard_map(shards, mesh=mesh, in_specs=in_specs, out_specs=out_specs, check_vma=False)
```

```python
import functools

import jax
import jax.numpy as jnp
from jax import lax
from jax.experimental import pallas as pl
from jax.experimental.pallas import tpu as pltpu
from jax.sharding import PartitionSpec as P

CHANNELS = 8
TAPS = 33
HALF = TAPS // 2
SIDE = 128
ROWS = 16
COLS = 32
PEERS = COLS // 2
SUB = SIDE // ROWS
MIXED = CHANNELS - 1
F32 = jnp.float32
BAND_ORDER = [2 * step + half for half in range(2) for step in range(ROWS // 2)]
BF16 = jnp.bfloat16
VMEM = pl.BlockSpec(memory_space=pltpu.VMEM)
SMEM = pl.BlockSpec(memory_space=pltpu.SMEM)
ANY = pl.BlockSpec(memory_space=pl.ANY)
HBM = pl.BlockSpec(memory_space=pltpu.HBM)
PARAMS = pltpu.CompilerParams(vmem_limit_bytes=24 * 1024 * 1024)


def reach(channel):
    return max(1, 2**channel * HALF // SIDE)


def blocks(channel):
    return 2 * reach(channel) + 1


def split(values):
    high = values.astype(BF16)
    low = (values - high.astype(F32)).astype(BF16)
    return high, low


def pair_rows(first, second):
    return jnp.concatenate(
        [first.reshape(ROWS, SUB, SIDE), second.reshape(ROWS, SUB, SIDE)], axis=1
    )


def unpair_rows(pairs):
    values = pairs.astype(F32)
    return (
        values[:, :SUB, :].reshape(SIDE, SIDE),
        values[:, SUB:, :].reshape(SIDE, SIDE),
    )


def along_rows(values):
    return jnp.concatenate(
        [values[SUB * p : SUB * p + SUB] for p in (b % 2 * (ROWS // 2) + b // 2 for b in range(ROWS))],
        axis=0,
    )


def along_peers(values):
    return jnp.concatenate(
        [values[SUB * b : SUB * b + SUB] for b in BAND_ORDER], axis=0
    )


def scaled(values, scale):
    return (values.reshape(ROWS, SUB, SIDE) * scale).reshape(SIDE, SIDE)


def fetch(sources, targets, sem):
    copies = [
        pltpu.make_async_copy(source, target, sem.at[number])
        for number, (source, target) in enumerate(zip(sources, targets))
    ]
    for copy in copies:
        copy.start()
    for copy in copies:
        copy.wait()


def scatter_round(values, place):
    near = values.astype(BF16).astype(F32)
    step = (near * (1.0 + 0.7 / 128)).astype(BF16).astype(F32) - near
    row = lax.broadcasted_iota(jnp.int32, values.shape, 0).astype(F32)
    column = lax.broadcasted_iota(jnp.int32, values.shape, 1).astype(F32)
    mixed = row * 0.7548777 + column * 0.5698403 + place.astype(F32) * 0.6180340
    return (values + step * (mixed - jnp.floor(mixed) - 0.5)).astype(BF16)


def source_kernel(place_ref, region_ref, fill_in, height_in, density_in, out_ref, *scratch):
    fill_ref, height_ref, density_ref, sem = scratch
    fetch((fill_in, height_in, density_in), (fill_ref, height_ref, density_ref), sem)
    fill = fill_ref[region_ref[0, 0]]
    height = height_ref[...]
    source = (density_ref[...] + fill) * height
    turned = source.T.astype(BF16)
    rounded = scatter_round(height, place_ref[0])
    for peer in range(PEERS):
        out_ref[peer, :SIDE, :] = turned
        out_ref[peer, SIDE:, :] = rounded


def toeplitz(taps_ref, channel, direction, merged):
    width = (blocks(channel) + 1) * SIDE
    lane = lax.broadcasted_iota(jnp.int32, (1, SIDE), 1)
    parts = [jnp.zeros((1, SIDE), F32) for _ in range(width // SIDE)]
    for position in range(TAPS):
        value = taps_ref[channel, position]
        if merged and position == 0:
            continue
        if merged and position == TAPS - 1:
            value = value + taps_ref[channel, 0]
        place = reach(channel) * SIDE + direction * (position - HALF) * 2**channel
        part, inside = divmod(place, SIDE)
        parts[part] = jnp.where(lane == inside, value, parts[part])
    base = jnp.concatenate(parts, axis=1).astype(BF16).astype(F32)
    spread = jnp.broadcast_to(base, (SIDE, width))
    rolled = pltpu.roll(spread, 0, 1, stride=1, stride_axis=0)
    return rolled[:, : blocks(channel) * SIDE].astype(BF16)


def fill_tables(taps_ref, outs, last_ref, direction, merged):
    for channel in range(MIXED):
        outs[channel][...] = toeplitz(taps_ref, channel, direction, merged and channel == 6)
    steps = last_ref.shape[0]
    for step in range(steps):
        places = [t for t in range(TAPS) if (direction * (t - HALF) + HALF - step) % steps == 0]
        value = taps_ref[MIXED, places[0]]
        for place in places[1:]:
            value = value + taps_ref[MIXED, place]
        last_ref[step] = jnp.full((SUB, SIDE), value, F32).astype(BF16).astype(F32)


def tables_kernel(col_in, row_in, gains_in, rates_in, after_ref, *refs):
    scales_ref, col_ref, row_ref, gains_ref, rates_ref, sem = refs[2 * MIXED + 2 :]
    fetch(
        (col_in, row_in, gains_in, rates_in), (col_ref, row_ref, gains_ref, rates_ref), sem
    )
    for number in range(CHANNELS):
        scales_ref[number] = jnp.full((SUB, SIDE), gains_ref[number], F32)
        scales_ref[CHANNELS + number] = jnp.full((SUB, SIDE), rates_ref[number], F32)
    fill_tables(col_ref, refs[:MIXED], refs[MIXED], -1, False)
    fill_tables(row_ref, refs[MIXED + 1 : 2 * MIXED + 1], refs[2 * MIXED + 1], 1, True)


def smooth_kernel(place_ref, class_ref, own_ref, other_ref, height_in, target_in, last_ref, *refs):
    tables, out_ref = refs[:MIXED], refs[MIXED]
    window_ref, height_ref, target_ref, sem = refs[MIXED + 1 :]
    copies = [
        pltpu.make_async_copy(height_in, height_ref, sem.at[0]),
        pltpu.make_async_copy(target_in, target_ref, sem.at[1]),
    ]
    for copy in copies:
        copy.start()
    here = place_ref[0]
    last = jnp.zeros((SIDE, SIDE), F32)
    for step in range(COLS):
        block = lax.rem(here + (COLS - HALF + step), COLS) // 2
        chunk_ref = own_ref if step % 2 == 0 else other_ref
        values = chunk_ref[block, :SIDE, :]
        window_ref[step * SIDE : (step + 1) * SIDE, :] = values
        last = last + scaled(values.astype(F32), last_ref[step])
    smoothed = []
    for channel in range(MIXED):
        first = (HALF - reach(channel)) * SIDE
        smoothed.append(
            jnp.dot(
                tables[channel][...],
                window_ref[first : first + blocks(channel) * SIDE, :],
                preferred_element_type=F32,
            )
        )
    smoothed.append(last)
    for pair in range(CHANNELS // 2):
        out_ref[:, 16 * pair : 16 * pair + 16, :] = pair_rows(
            smoothed[2 * pair], smoothed[2 * pair + 1]
        ).astype(BF16)
    for copy in copies:
        copy.wait()
    away = (height_ref[...] - target_ref[...]).T
    high, low = split(away)
    row = lax.broadcasted_iota(jnp.int32, (SIDE, SIDE), 0)
    lane = lax.broadcasted_iota(jnp.int32, (SIDE, SIDE), 1)
    first = (row % SUB == 0) & (lane == 0)
    low = jnp.where(first, class_ref[0, 0].astype(F32), low.astype(F32))
    out_ref[:, 64:, :] = pair_rows(high.astype(F32), low).astype(BF16)


def rolled_rows(values, block_shift):
    shift = block_shift * SUB % SIDE
    if shift == 0:
        return values
    return jnp.concatenate([values[SIDE - shift :], values[: SIDE - shift]], axis=0)


def pressure_kernel(scales_ref, long_ref, last_ref, *refs):
    tables, out_ref, gain_ref = refs[:MIXED], refs[MIXED], refs[MIXED + 1]
    smoothed = []
    for pair in range(CHANNELS // 2):
        for values in unpair_rows(long_ref[:, 16 * pair : 16 * pair + 16, :]):
            smoothed.append(along_rows(values))
    high, low = map(along_rows, unpair_rows(long_ref[:, 64:, :]))
    low = low.reshape(ROWS, SUB, SIDE)
    row = lax.broadcasted_iota(jnp.int32, (ROWS, SUB, SIDE), 1)
    lane = lax.broadcasted_iota(jnp.int32, (ROWS, SUB, SIDE), 2)
    first = (row == 0) & (lane == 0)
    kind = jnp.max(jnp.where(first, low, 0.0), axis=(1, 2), keepdims=True)
    away = high + jnp.where(first, 0.0, low).reshape(SIDE, SIDE)
    rate = jnp.zeros((ROWS, SUB, SIDE), F32)
    for number in range(CHANNELS):
        rate = jnp.where(kind == float(number), scales_ref[CHANNELS + number], rate)
    rate = rate.reshape(SIDE, SIDE)

    pressure = jnp.zeros((SIDE, SIDE), F32)
    for channel in range(MIXED):
        spread = jnp.dot(
            smoothed[channel].astype(BF16), tables[channel][...], preferred_element_type=F32
        )
        total = None
        for block in range(blocks(channel)):
            term = rolled_rows(
                spread[:, block * SIDE : (block + 1) * SIDE], block - reach(channel)
            )
            total = term if total is None else total + term
        pressure = pressure + scaled(total, scales_ref[channel])
    total = jnp.zeros((SIDE, SIDE), F32)
    for step in range(ROWS):
        total = total + rolled_rows(scaled(smoothed[MIXED], last_ref[step]), step)
    pressure = pressure + scaled(total, scales_ref[MIXED])

    shifted = 1.0 + pressure
    decay = jnp.exp(-jnp.abs(shifted))
    removed = rate * (jnp.maximum(shifted, 0.0) + jnp.log1p(decay))
    slope = jnp.where(shifted >= 0, 1.0, decay) / (1.0 + decay)
    adjoint = (-(away - removed) * rate * slope / SIDE).astype(BF16)

    weighted = []
    gain_rows = []
    for channel in range(CHANNELS):
        total = jnp.zeros((SIDE, SIDE), F32)
        if channel < MIXED:
            for block in range(blocks(channel)):
                term = lax.dot_general(
                    adjoint,
                    tables[channel][:, block * SIDE : (block + 1) * SIDE],
                    (((1,), (1,)), ((), ())),
                    preferred_element_type=F32,
                )
                total = total + rolled_rows(term, reach(channel) - block)
        else:
            wide = adjoint.astype(F32)
            for step in range(ROWS):
                total = total + rolled_rows(scaled(wide, last_ref[step]), -step)
        gain_rows.append(jnp.sum(total * smoothed[channel], axis=0, keepdims=True))
        weighted.append(scaled(total, scales_ref[channel]))
    for pair in range(CHANNELS // 2):
        out_ref[:, 16 * pair : 16 * pair + 16, :] = pair_rows(
            along_peers(weighted[2 * pair]), along_peers(weighted[2 * pair + 1])
        ).astype(BF16)
    high, low = split(along_peers(removed))
    out_ref[:, 64:, :] = pair_rows(high.astype(F32), low.astype(F32)).astype(BF16)
    gain_ref[...] = jnp.concatenate(gain_rows, axis=0)


def gradient_kernel(
    place_ref, region_ref, back_ref, own_ref, other_ref, gain_ref, last_ref, *refs
):
    tables, sums_ref = refs[:MIXED], refs[MIXED]
    weighted = []
    for pair in range(CHANNELS // 2):
        weighted.extend(unpair_rows(back_ref[:, 16 * pair : 16 * pair + 16, :]))
    turned = weighted[MIXED].T
    narrow = [weighted[channel].astype(BF16) for channel in range(MIXED)]
    here = place_ref[0]
    parts = []
    for step in range(COLS):
        block = lax.rem(here + (COLS - HALF + step), COLS) // 2
        values = (own_ref if step % 2 == 0 else other_ref)[block, SIDE:, :]
        product = turned * values.astype(F32)
        product = jnp.sum(product.reshape(ROWS, SUB, SIDE), axis=0)
        terms = product * last_ref[step]
        ahead = step - HALF
        channels = [c for c in range(MIXED) if abs(ahead) <= reach(c)]
        for channel in channels:
            first = (ahead + reach(channel)) * SIDE
            cross = jnp.dot(narrow[channel], values, preferred_element_type=F32)
            taps = tables[channel][:, first : first + SIDE].astype(F32)
            terms = terms + jnp.sum((cross * taps).reshape(ROWS, SUB, SIDE), axis=0)
        parts.append(terms)
    total = jnp.sum(jnp.concatenate(parts, axis=0), axis=1, keepdims=True)
    row = lax.broadcasted_iota(jnp.int32, (COLS * SUB, SIDE), 0)
    lane = lax.broadcasted_iota(jnp.int32, (COLS * SUB, SIDE), 1)
    block = lax.rem(here + HALF + row // SUB, COLS)
    line = jnp.sum(jnp.where(lane == block, total, 0.0), axis=0, keepdims=True)
    gain = jnp.sum(gain_ref[...], axis=1, keepdims=True)
    gain = jnp.where(lane[:SUB] == COLS + row[:SUB], gain, 0.0)
    region = region_ref[0, 0].astype(F32)
    line = line + jnp.sum(gain, axis=0, keepdims=True)
    line = line + jnp.where(lane[:1] == 2 * COLS, region, 0.0)
    for peer in range(COLS):
        sums_ref[peer] = line


def band_kernel(lines_ref, out_ref):
    lines = lines_ref[...].reshape(COLS, SIDE)
    row = lax.broadcasted_iota(jnp.int32, (COLS, SIDE), 0)
    lane = lax.broadcasted_iota(jnp.int32, (COLS, SIDE), 1)
    band = jnp.sum(lines, axis=0, keepdims=True)
    sender = 2 * (row % PEERS) + row // PEERS
    held = jnp.sum(jnp.where(lane == sender, band, 0.0), axis=1, keepdims=True)
    region = jnp.sum(jnp.where(lane == 2 * COLS, lines, 0.0), axis=1, keepdims=True)
    fill = jnp.where(region == lane.astype(F32), held, 0.0)
    both = jnp.concatenate([jnp.sum(fill, axis=0, keepdims=True), band], axis=0)
    for peer in range(ROWS):
        out_ref[peer] = both


def total_kernel(bands_ref, back_ref, height_ref, new_ref, fill_ref, gain_ref):
    total = jnp.sum(bands_ref[...], axis=0)
    fill_ref[...] = total[0]
    gain_ref[...] = total[1, COLS : COLS + CHANNELS]
    high, low = unpair_rows(back_ref[:, 64:80, :])
    new_ref[...] = height_ref[...] - (high + low).T


def shape(*dims, dtype=F32):
    return jax.ShapeDtypeStruct(dims, dtype)


def shards(
    height,
    density,
    target,
    region_of_block,
    class_of_block,
    fill_level,
    rates,
    col_taps,
    row_taps,
    gains,
):
    place = lax.axis_index("col").astype(jnp.int32).reshape(1)
    copies = pl.pallas_call(
        source_kernel,
        out_shape=shape(PEERS, 2 * SIDE, SIDE, dtype=BF16),
        in_specs=[SMEM, SMEM, HBM, HBM, HBM],
        out_specs=VMEM,
        scratch_shapes=[
            pltpu.SMEM((SIDE,), F32),
            pltpu.VMEM((SIDE, SIDE), F32),
            pltpu.VMEM((SIDE, SIDE), F32),
            pltpu.SemaphoreType.DMA((3,)),
        ],
        compiler_params=pltpu.CompilerParams(vmem_limit_bytes=60 * 1024 * 1024),
        name="source",
    )(place, region_of_block, fill_level, height, density)
    groups = [[2 * block + core for block in range(PEERS)] for core in range(2)]
    own = lax.all_to_all(copies, "col", 0, 0, axis_index_groups=groups, tiled=True)
    other = lax.ppermute(own, "col", [(block, block ^ 1) for block in range(COLS)])
    table_shapes = [shape(SIDE, blocks(c) * SIDE, dtype=BF16) for c in range(MIXED)]
    made = pl.pallas_call(
        tables_kernel,
        out_shape=table_shapes
        + [shape(COLS, SUB, SIDE)]
        + table_shapes
        + [shape(ROWS, SUB, SIDE), shape(2 * CHANNELS, SUB, SIDE)],
        in_specs=[HBM] * 4 + [ANY],
        out_specs=[VMEM] * (2 * MIXED + 3),
        scratch_shapes=[
            pltpu.SMEM((CHANNELS, TAPS), F32),
            pltpu.SMEM((CHANNELS, TAPS), F32),
            pltpu.SMEM((CHANNELS,), F32),
            pltpu.SMEM((CHANNELS,), F32),
            pltpu.SemaphoreType.DMA((4,)),
        ],
        compiler_params=PARAMS,
        cost_estimate=pl.CostEstimate(flops=4000000, bytes_accessed=4000000, transcendentals=0),
        name="tables",
    )(col_taps, row_taps, gains, rates, own)
    col_tables, col_last = made[:MIXED], made[MIXED]
    row_tables, row_last = made[MIXED + 1 : 2 * MIXED + 1], made[2 * MIXED + 1]
    scales = made[2 * MIXED + 2]

    smoothed = pl.pallas_call(
        smooth_kernel,
        out_shape=shape(ROWS, 80, SIDE, dtype=BF16),
        in_specs=[SMEM, SMEM, VMEM, VMEM, HBM, HBM] + [VMEM] * (1 + MIXED),
        out_specs=VMEM,
        scratch_shapes=[
            pltpu.VMEM((COLS * SIDE, SIDE), BF16),
            pltpu.VMEM((SIDE, SIDE), F32),
            pltpu.VMEM((SIDE, SIDE), F32),
            pltpu.SemaphoreType.DMA((2,)),
        ],
        compiler_params=PARAMS,
        name="smooth",
    )(place, class_of_block, own, other, height, target, col_last, *col_tables)
    long = lax.all_to_all(smoothed, "row", 0, 0, axis_index_groups=[BAND_ORDER], tiled=True)

    back, gain_part = pl.pallas_call(
        pressure_kernel,
        out_shape=[shape(ROWS, 80, SIDE, dtype=BF16), shape(CHANNELS, SIDE)],
        in_specs=[VMEM] * (3 + MIXED),
        out_specs=[VMEM, VMEM],
        compiler_params=PARAMS,
        name="pressure",
    )(scales, long, row_last, *row_tables)
    tile = lax.all_to_all(back, "row", 0, 0, axis_index_groups=[BAND_ORDER], tiled=True)
    lines = pl.pallas_call(
        gradient_kernel,
        out_shape=shape(COLS, 1, SIDE),
        in_specs=[SMEM, SMEM] + [VMEM] * (5 + MIXED),
        out_specs=VMEM,
        compiler_params=PARAMS,
        name="gradient",
    )(place, region_of_block, tile, own, other, gain_part, col_last, *col_tables)
    by_col = lax.all_to_all(
        lines, "col", 0, 0, axis_index_groups=[groups[0] + groups[1]], tiled=True
    )
    bands = pl.pallas_call(
        band_kernel,
        out_shape=shape(ROWS, 2, SIDE),
        in_specs=[VMEM],
        out_specs=VMEM,
        compiler_params=PARAMS,
        name="band",
    )(by_col)
    by_row = lax.all_to_all(bands, "row", 0, 0, axis_index_groups=[BAND_ORDER], tiled=True)
    new_height, fill_grad, gain_grad = pl.pallas_call(
        total_kernel,
        out_shape=[shape(SIDE, SIDE), shape(SIDE), shape(CHANNELS)],
        in_specs=[VMEM] * 3,
        out_specs=[VMEM] * 3,
        compiler_params=PARAMS,
        name="total",
    )(by_row, tile, height)
    return new_height, gain_grad, fill_grad


def solution(mesh):
    cells = P("row", "col")
    in_specs = (cells,) * 5 + (P(),) * 5
    out_specs = (cells, P(), P())
    return jax.shard_map(shards, mesh=mesh, in_specs=in_specs, out_specs=out_specs, check_vma=False)
```
